512 devices in a mesh: dp: 32 (over y_hi, z, core), fsdp: 16 (over y_lo, x).
Axes of the slice: x: 4, y: 8 (y_hi: 2, y_lo: 4; y = y_hi * 4 + y_lo), z: 8, core: 2. Of those that a mesh axis runs over, the one named last changes fastest.
Arguments:
- state0: float32 [65536, 2640], P(('dp', 'fsdp')), may hold values from -6 to 6
- injected: bfloat16 [65536, 2640], P(('dp', 'fsdp')), may hold values from -6 to 6
- core_weight: bfloat16 [2640, 2640], P('fsdp'), may hold values from -0.125 to 0.125
- gain: float32 [2640], replicated, may hold values from 0.1 to 1.9
- counts: int32 [512], P(('dp', 'fsdp')), may hold values from 1 to 2, as said below
- cotangent: float32 [65536, 2640], P(('dp', 'fsdp')), may hold values from -6 to 6
Outputs:
- final_state: bfloat16 [65536, 2640], P(('dp', 'fsdp'))
- injected_grad: bfloat16 [65536, 2640], P(('dp', 'fsdp'))
- gain_grad: float32 [2640], replicated
The draws below stay inside these ranges and needn't reach their ends.
Inputs may be any that keep to these rules, and one draw needn't show every extreme that they name: Group j runs counts[j] iterations; in every draw some group runs 2 and some group runs 1.
All inputs are finite; a program needn't handle non-finite values.
Results may differ from the reference program's by a relative error of at most 0.0045.
Values may be sent and summed in bfloat16 or wider, within the bound.
No kernel may reach another device: no remote copies, remote signals or barrier semaphores. Data moves between devices by JAX's collectives and lax.ppermute only.
A program may use at most 128 MiB of HBM per device.

```python
import jax
import jax.numpy as jnp
from jax import lax

W = 2640
ROUNDS_MAX = 2
TOK_DEV = 128
TOKENS = 65536
N_DP = 32
N_FSDP = 16


def draw_counts(key, part):
    key = jax.random.fold_in(key, 7)
    first_key, second_key = jax.random.split(key)
    group_count = N_DP * N_FSDP
    base = jax.random.randint(first_key, (group_count,), 1, ROUNDS_MAX + 1)
    order = jax.random.permutation(second_key, group_count)
    base = base.at[order[0]].set(ROUNDS_MAX)
    base = base.at[order[1]].set(1)
    return base.astype(jnp.int32)


def shard_levels(key, dims, shards, low, top_value):
    level, own = 1.0, jax.random.fold_in(key, 6)
    for dim, blocks in shards:
        heights = jnp.exp(jax.random.uniform(jax.random.fold_in(own, dim), (blocks,), jnp.float32, low / len(shards), top_value / len(shards)))
        level = level * jnp.repeat(heights, dims[dim] // blocks).reshape([-1 if axis == dim else 1 for axis in range(len(dims))])
    return level


def gaussian(stream_key, shape, spread, bound, pieces=(), dtype=jnp.bfloat16):
    factor_of = shard_levels(stream_key, shape, pieces, -0.22, 0.18) if pieces else 1.0
    entries = jax.random.normal(stream_key, shape, jnp.float32) * spread * factor_of
    return jnp.minimum(jnp.maximum(entries, -bound), bound).astype(dtype)


def setup_inputs(seed: int = 0) -> dict:
    key_of = jax.random.split(jax.random.key(seed), 7)
    state0 = gaussian(key_of[0], (TOKENS, W), 1.0, 6.0, ((0, 512),), jnp.float32)
    injected = gaussian(key_of[1], (TOKENS, W), 1.0, 6.0, ((0, 512),))
    core_weight = gaussian(key_of[2], (W, W), W ** -0.5, 0.125, ((0, 16),))
    gain = jnp.clip(1.0 + 0.18 * jax.random.normal(key_of[3], (W,), jnp.float32), 0.1, 1.9)
    counts = draw_counts(jax.random.fold_in(key_of[6], 71), 0)
    cotangent = gaussian(key_of[5], (TOKENS, W), 1.0, 6.0, ((0, 512),), jnp.float32)
    return dict(state0=state0, injected=injected, core_weight=core_weight, gain=gain, counts=counts, cotangent=cotangent)


epsilon = 1e-06

def normalize(state):
    inv_rms = lax.rsqrt(lax.optimization_barrier(jnp.mean(state * state, axis=-1, keepdims=True)) + epsilon)
    return (state * inv_rms, inv_rms)

def advance(state, gain, weight, inject):
    normed_rows, inv_rms = normalize(state)
    operand = (normed_rows * gain).astype(jnp.bfloat16)
    return jnp.dot(operand, weight, preferred_element_type=jnp.float32) + inject.astype(jnp.float32)

def retreat(state, upstream, gain, weight):
    normed_rows, inv_rms = normalize(state)
    up_bf = upstream.astype(jnp.bfloat16)
    back_proj = lax.dot_general(up_bf, weight, (((1,), (1,)), ((), ())), preferred_element_type=jnp.float32)
    gain_part = lax.optimization_barrier(jnp.sum(back_proj * normed_rows, axis=0))
    scaled = back_proj * gain
    state_grad = inv_rms * (scaled - normed_rows * lax.optimization_barrier(jnp.mean(scaled * normed_rows, axis=-1, keepdims=True)))
    return (state_grad, gain_part)

def finish(start, first, inject, upstream, rounds, gain, weight):

    def step_once(step_index, states):
        earlier, before, latest = states
        return (before, latest, advance(latest, gain, weight, inject))
    earlier, before, latest = lax.fori_loop(1, rounds, step_once, (start, start, first))
    state_grad, gain_part = retreat(before, upstream, gain, weight)

    def deeper():
        unused, second_part = retreat(earlier, state_grad, gain, weight)
        return (gain_part + second_part, upstream + state_grad)

    def shallow():
        return (gain_part, upstream)
    total_part, inject_grad = lax.cond(rounds >= 2, deeper, shallow)
    return (latest.astype(jnp.bfloat16), inject_grad.astype(jnp.bfloat16), total_part)

def reference(state0, injected, core_weight, gain, counts, cotangent):
    group_count = N_DP * N_FSDP
    starts = state0.reshape(group_count, TOK_DEV, W)
    injects = injected.reshape(group_count, TOK_DEV, W)
    upstreams = cotangent.reshape(group_count, TOK_DEV, W)

    def one_group(packed):
        start, inject, upstream, rounds = packed
        first = advance(start, gain, core_weight, inject)
        return finish(start, first, inject, upstream, rounds, gain, core_weight)
    final_rows, inject_grad, parts = lax.map(one_group, (starts, injects, upstreams, counts))
    return (final_rows.reshape(TOKENS, W), inject_grad.reshape(TOKENS, W), lax.optimization_barrier(jnp.sum(parts, axis=0)))
```

```python
import itertools

import jax
import jax.numpy as jnp
from jax import lax
from jax.experimental import pallas as pl
from jax.experimental.pallas import tpu as pltpu
from jax.sharding import PartitionSpec as P

AXES = ("dp", "fsdp")
NX, NY, NZ, NC = 4, 8, 8, 2
YL = 4
W = 2640
SH = 165
SP = 176
WP = 16 * SP
HALF = WP // 2
TOK = 128
TILE = 256
EPS = 1e-06
BF = jnp.bfloat16
F32 = jnp.float32


def line(x, y, z, c):
    x, y, z, c = x % NX, y % NY, z % NZ, c % NC
    return ((y // YL) * NZ * NC + z * NC + c) * 16 + (y % YL) * NX + x


def chips():
    return itertools.product(range(NX), range(NY), range(NZ), range(NC))


def along(first, step):
    pairs = []
    for x, y, z, c in chips():
        in_x = (c == 0) == first
        pairs.append((line(x, y, z, c), line(x + step * in_x, y + step * (not in_x), z, c)))
    return pairs


SWAP = [(line(x, y, z, c), line(x, y, z, 1 - c)) for x, y, z, c in chips()]


def send(array, pairs):
    return lax.ppermute(array, AXES, pairs)


def nt(a, b):
    return lax.dot_general(a, b, (((1,), (1,)), ((), ())), preferred_element_type=F32)


def core_kernel(place, op0_ref, cb_ref, n0_ref, inj_ref, cot_ref, gain_ref, *rest):
    pieces = rest[:10]
    final_ref, injg_ref, part_ref = rest[10:13]
    w_ref, s1_ref, back_ref, op1_ref, db_ref, sems = rest[13:]
    px, py, pc, rounds = place[0], place[1], place[2], place[3]
    copies = []
    for who in range(2):
        core = pc if who == 0 else 1 - pc
        base = 5 * who
        for k in range(4):
            for j in range(4):
                sx = jnp.where(core == 0, px + 4 - j, px + 4 - k) % 4
                sy = jnp.where(core == 0, py + 4 - k, py + 4 - j) % 4
                row = pl.multiple_of((sy * 4 + sx) * SP, SP)
                if k == 0:
                    src = pieces[base].at[j]
                elif k == 1:
                    src = pieces[base + 1].at[j]
                elif k == 3:
                    src = pieces[base + 2].at[j]
                elif j < 2:
                    src = pieces[base + 3].at[j]
                else:
                    src = pieces[base + 4].at[j - 2]
                dst = w_ref.at[pl.ds(row, SP), pl.ds(pl.multiple_of(core * HALF, 128), HALF)]
                copies.append(pltpu.make_async_copy(src, dst, sems.at[len(copies)]))
    for c in copies:
        c.start()
    for c in copies:
        c.wait()
    deep = rounds >= 2

    def first(t, ssq):
        cols = pl.ds(pl.multiple_of(t * TILE, TILE), TILE)
        s1 = jnp.dot(op0_ref[...], w_ref[:, cols], preferred_element_type=F32) + inj_ref[:, cols].astype(F32)
        s1_ref[:, cols] = s1
        back_ref[:, cols] = nt(cb_ref[...], w_ref[cols, :])
        return ssq + jnp.sum(s1 * s1, axis=1, keepdims=True)

    ssq = lax.fori_loop(0, WP // TILE, first, jnp.zeros((TOK, 1), F32))
    inv1 = lax.rsqrt(ssq / W + EPS)

    def second(t, dots):
        cols = pl.ds(pl.multiple_of(t * TILE, TILE), TILE)
        n1 = s1_ref[:, cols] * inv1
        back = back_ref[:, cols]
        gain = gain_ref[:, cols]
        op1_ref[:, cols] = (n1 * gain).astype(BF)
        v = jnp.where(deep, n1, n0_ref[:, cols])
        part_ref[:, cols] = jnp.sum(back * v, axis=0, keepdims=True)
        return dots + jnp.sum(back * gain * n1, axis=1, keepdims=True)

    dots = lax.fori_loop(0, WP // TILE, second, jnp.zeros((TOK, 1), F32))
    mean1 = dots / W

    def third(t, carry):
        cols = pl.ds(pl.multiple_of(t * TILE, TILE), TILE)
        n1 = s1_ref[:, cols] * inv1
        d1 = inv1 * (back_ref[:, cols] * gain_ref[:, cols] - n1 * mean1)
        db_ref[:, cols] = d1.astype(BF)
        cot = cot_ref[:, cols]
        injg_ref[:, cols] = jnp.where(deep, cot + d1, cot).astype(BF)
        return carry

    lax.fori_loop(0, WP // TILE, third, 0)

    def fourth(t, carry):
        cols = pl.ds(pl.multiple_of(t * TILE, TILE), TILE)
        s2 = jnp.dot(op1_ref[...], w_ref[:, cols], preferred_element_type=F32) + inj_ref[:, cols].astype(F32)
        final_ref[:, cols] = jnp.where(deep, s2, s1_ref[:, cols]).astype(BF)
        back = nt(db_ref[...], w_ref[cols, :])
        part2 = jnp.sum(back * n0_ref[:, cols], axis=0, keepdims=True)
        part_ref[:, cols] += jnp.where(deep, part2, jnp.zeros_like(part2))
        return carry

    lax.fori_loop(0, WP // TILE, fourth, 0)


def core_call(place, op0, cb, n0, inj, cot, gain, pieces):
    vm = pl.BlockSpec(memory_space=pltpu.VMEM)
    return pl.pallas_call(
        core_kernel,
        out_shape=(
            jax.ShapeDtypeStruct((TOK, WP), BF),
            jax.ShapeDtypeStruct((TOK, WP), BF),
            jax.ShapeDtypeStruct((1, WP), F32),
        ),
        in_specs=[pl.BlockSpec(memory_space=pltpu.SMEM)] + [vm] * 6 + [pl.BlockSpec(memory_space=pl.ANY)] * 10,
        out_specs=(vm, vm, vm),
        scratch_shapes=[
            pltpu.VMEM((WP, WP), BF),
            pltpu.VMEM((TOK, WP), F32),
            pltpu.VMEM((TOK, WP), F32),
            pltpu.VMEM((TOK, WP), BF),
            pltpu.VMEM((TOK, WP), BF),
            pltpu.SemaphoreType.DMA((32,)),
        ],
        compiler_params=pltpu.CompilerParams(vmem_limit_bytes=48 * 2**20),
        cost_estimate=pl.CostEstimate(flops=8 * TOK * WP * WP, bytes_accessed=2 * WP * WP, transcendentals=0),
    )(place, op0, cb, n0, inj, cot, gain, *pieces)


def widen(array):
    flipped = array.T.reshape(16, SH, TOK)
    return jnp.pad(flipped, ((0, 0), (0, SP - SH), (0, 0))).reshape(WP, TOK).T


def narrow(array):
    return array.T.reshape(16, SP, -1)[:, :SH].reshape(W, -1).T


def gather(weight, pc):
    wide = jnp.pad(weight.reshape(SH, 16, SH), ((0, SP - SH), (0, 0), (0, SP - SH))).reshape(SP, WP)
    own = jnp.where(pc == 0, wide[:, :HALF], wide[:, HALF:])
    m1 = send(own, along(True, 1))
    m3 = send(own, along(True, -1))
    m2 = send(m1, along(True, 1))
    row = jnp.stack([own, m1, m2, m3])
    n1 = send(row, along(False, 1))
    n3 = send(row, along(False, -1))
    n2a = send(n1[:2], along(False, 1))
    n2b = send(n3[2:], along(False, -1))
    mine = (row, n1, n3, n2a, n2b)
    return mine + tuple(send(a, SWAP) for a in mine)


def total(part):
    dp_groups = [[yh * 16 + z * 2 + c for z in range(8) for c in range(2)] for yh in range(2)]
    got = lax.all_to_all(jnp.broadcast_to(part, (16, WP)), "dp", 0, 0, axis_index_groups=dp_groups)
    part = jnp.sum(got.reshape(16, WP), axis=0, keepdims=True)
    planes = [[line(x, y, z, c) for y in range(NY) for x in range(NX)] for z in range(NZ) for c in range(NC)]
    got = lax.all_to_all(jnp.broadcast_to(part, (32, WP)), AXES, 0, 0, axis_index_groups=planes)
    return jnp.sum(got.reshape(32, WP), axis=0, keepdims=True)


def shards(state0, injected, core_weight, gain, counts, cotangent):
    dp, fs = lax.axis_index("dp"), lax.axis_index("fsdp")
    pc = dp % 2
    place = jnp.stack([fs % 4, fs // 4, pc, counts[0]]).astype(jnp.int32)
    pieces = gather(core_weight, pc)
    gain_w = widen(jnp.broadcast_to(gain, (TOK, W)))[:1]
    start = widen(state0)
    inv = lax.rsqrt(jnp.sum(start * start, axis=-1, keepdims=True) / W + EPS)
    n0 = start * inv
    op0 = (n0 * gain_w).astype(BF)
    cot = widen(cotangent)
    final, injg, part = core_call(place, op0, cot.astype(BF), n0, widen(injected), cot, gain_w, pieces)
    return (narrow(final), narrow(injg), narrow(total(part)).reshape(W))


def solution(mesh):
    rows = P(AXES, None)
    return jax.shard_map(
        shards,
        mesh=mesh,
        in_specs=(rows, rows, P("fsdp", None), P(), P(AXES), rows),
        out_specs=(rows, rows, P()),
        check_vma=False,
    )
```

```python
import itertools

import jax
import jax.numpy as jnp
from jax import lax
from jax.experimental import pallas as pl
from jax.experimental.pallas import tpu as pltpu
from jax.sharding import PartitionSpec as P

AXES = ("dp", "fsdp")
NX, NY, NZ, NC = 4, 8, 8, 2
YL = 4
W = 2640
SH = 165
SP = 176
WP = 16 * SP
HALF = WP // 2
TOK = 128
TILE = 256
EPS = 1e-06
BF = jnp.bfloat16
F32 = jnp.float32


def line(x, y, z, c):
    x, y, z, c = x % NX, y % NY, z % NZ, c % NC
    return ((y // YL) * NZ * NC + z * NC + c) * 16 + (y % YL) * NX + x


def chips():
    return itertools.product(range(NX), range(NY), range(NZ), range(NC))


def along(first, step):
    pairs = []
    for x, y, z, c in chips():
        in_x = (c == 0) == first
        pairs.append((line(x, y, z, c), line(x + step * in_x, y + step * (not in_x), z, c)))
    return pairs


SWAP = [(line(x, y, z, c), line(x, y, z, 1 - c)) for x, y, z, c in chips()]


def send(array, pairs):
    return lax.ppermute(array, AXES, pairs)


def nt(a, b):
    return lax.dot_general(a, b, (((1,), (1,)), ((), ())), preferred_element_type=F32)


def spread_kernel(place, w_ref, out_ref, wide_ref):
    wide_ref[...] = jnp.zeros_like(wide_ref)
    for t in range(20):
        wide_ref[0:SH, 128 * t : 128 * t + 128] = w_ref[:, 128 * t : 128 * t + 128].astype(F32)
    wide_ref[0:SH, 2560:W] = w_ref[:, 2560:W].astype(F32)
    lane = lax.broadcasted_iota(jnp.int32, (SP, 128), 1)
    for core in range(2):

        @pl.when(place[2] == core)
        def _():
            for t in range(HALF // 128):
                tile = jnp.zeros((SP, 128), F32)
                for j in range(8):
                    low, high = SP * j - 128 * t, SP * j + SH - 128 * t
                    if high <= 0 or low >= 128:
                        continue
                    q = SH * (8 * core + j) - low
                    base = (q // 128) * 128
                    win = wide_ref[:, base : base + 256]
                    moved = pltpu.roll(win, (base - q) % 256, 1)[:, :128]
                    tile = jnp.where((lane >= low) & (lane < high), moved, tile)
                out_ref[:, 128 * t : 128 * t + 128] = tile.astype(BF)

def spread(place, w):
    vm = pl.BlockSpec(memory_space=pltpu.VMEM)
    return pl.pallas_call(
        spread_kernel,
        out_shape=jax.ShapeDtypeStruct((SP, HALF), BF),
        in_specs=[pl.BlockSpec(memory_space=pltpu.SMEM), vm],
        out_specs=vm,
        scratch_shapes=[pltpu.VMEM((SP, 2944), F32)],
        compiler_params=pltpu.CompilerParams(vmem_limit_bytes=16 * 2**20),
    )(place, w)

def prepare_kernel(state_ref, inj_ref, cot_ref, gain_ref, n0_ref, op0_ref, injw_ref, cotw_ref, cb_ref, wide_ref, tall_ref):
    def regroup(src_ref):
        for s in range(16):
            wide_ref[SP * s : SP * s + SH, :] = src_ref[SH * s : SH * s + SH, :]

    for s in range(16):
        wide_ref[SP * s + SH : SP * s + SP, :] = jnp.zeros((SP - SH, TOK), F32)
    regroup(state_ref)
    acc = jnp.zeros((TOK, 128), F32)
    for t in range(WP // 128):
        cols = slice(128 * t, 128 * t + 128)
        s = wide_ref[cols, :].T
        n0_ref[:, cols] = s
        acc = acc + s * s
    inv = lax.rsqrt(jnp.sum(acc, axis=1, keepdims=True) / W + EPS)
    for t in range(WP // 128):
        cols = slice(128 * t, 128 * t + 128)
        n0 = n0_ref[:, cols] * inv
        n0_ref[:, cols] = n0
        op0_ref[:, cols] = (n0 * gain_ref[:, cols]).astype(BF)
    regroup(cot_ref)
    for t in range(WP // 128):
        cols = slice(128 * t, 128 * t + 128)
        c = wide_ref[cols, :].T
        cotw_ref[:, cols] = c
        cb_ref[:, cols] = c.astype(BF)
    tall_ref[...] = inj_ref[...].astype(F32)
    regroup(tall_ref)
    for t in range(WP // 128):
        cols = slice(128 * t, 128 * t + 128)
        injw_ref[:, cols] = wide_ref[cols, :].T.astype(BF)

def prepare(state, inj, cot, gain):
    vm = pl.BlockSpec(memory_space=pltpu.VMEM)
    wide = lambda dt: jax.ShapeDtypeStruct((TOK, WP), dt)
    return pl.pallas_call(
        prepare_kernel,
        out_shape=(wide(F32), wide(BF), wide(BF), wide(F32), wide(BF)),
        in_specs=[vm] * 4,
        out_specs=(vm,) * 5,
        scratch_shapes=[pltpu.VMEM((WP, TOK), F32), pltpu.VMEM((W, TOK), F32)],
        compiler_params=pltpu.CompilerParams(vmem_limit_bytes=24 * 2**20),
        cost_estimate=pl.CostEstimate(flops=10**6, bytes_accessed=10**7, transcendentals=0),
    )(state.T, inj.T, cot.T, gain)


SINGLE = 2
SLOT = (0, 1, None, 2)


def core_kernel(place, op0_ref, cb_ref, n0_ref, inj_ref, cot_ref, gain_ref, *rest):
    pieces = rest[:16]
    final_ref, injg_ref, part_ref = rest[16:19]
    w_ref, s1_ref, back_ref, op1_ref, db_ref, sems = rest[19:]
    px, py, pc, rounds = place[0], place[1], place[2], place[3]
    copies = []
    for who in range(2):
        core = pc if who == 0 else 1 - pc
        for k in range(4):
            for j in range(4):
                sx = jnp.where(core == 0, px + 4 - j, px + 4 - k) % 4
                sy = jnp.where(core == 0, py + 4 - k, py + 4 - j) % 4
                row = pl.multiple_of((sy * 4 + sx) * SP, SP)
                src = pieces[8 * who + 2 * k + (j == SINGLE)]
                if j != SINGLE:
                    src = src.at[SLOT[j]]
                dst = w_ref.at[pl.ds(row, SP), pl.ds(pl.multiple_of(core * HALF, 128), HALF)]
                copies.append(pltpu.make_async_copy(src, dst, sems.at[len(copies)]))
    for c in copies:
        c.start()
    for c in copies:
        c.wait()
    deep = rounds >= 2

    def first(t, ssq):
        cols = pl.ds(pl.multiple_of(t * HALF, 128), HALF)
        back_ref[:, cols] = nt(cb_ref[...], w_ref[cols, :])
        s1 = jnp.dot(op0_ref[...], w_ref[:, cols], preferred_element_type=F32) + inj_ref[:, cols].astype(F32)
        s1_ref[:, cols] = s1
        return ssq + jnp.sum(s1 * s1, axis=1, keepdims=True)

    ssq = lax.fori_loop(0, 2, first, jnp.zeros((TOK, 1), F32))
    inv1 = lax.rsqrt(ssq / W + EPS)

    def second(t, dots):
        cols = pl.ds(pl.multiple_of(t * TILE, TILE), TILE)
        n1 = s1_ref[:, cols] * inv1
        back = back_ref[:, cols]
        gain = gain_ref[:, cols]
        op1_ref[:, cols] = (n1 * gain).astype(BF)
        v = jnp.where(deep, n1, n0_ref[:, cols])
        part_ref[:, cols] = jnp.sum(back * v, axis=0, keepdims=True)
        return dots + jnp.sum(back * gain * n1, axis=1, keepdims=True)

    dots = lax.fori_loop(0, WP // TILE, second, jnp.zeros((TOK, 1), F32))
    mean1 = dots / W

    def third(t, carry):
        cols = pl.ds(pl.multiple_of(t * TILE, TILE), TILE)
        n1 = s1_ref[:, cols] * inv1
        d1 = inv1 * (back_ref[:, cols] * gain_ref[:, cols] - n1 * mean1)
        db_ref[:, cols] = d1.astype(BF)
        cot = cot_ref[:, cols]
        injg_ref[:, cols] = jnp.where(deep, cot + d1, cot).astype(BF)
        return carry

    lax.fori_loop(0, WP // TILE, third, 0)

    def fourth(t, carry):
        cols = pl.ds(pl.multiple_of(t * HALF, 128), HALF)
        s2 = jnp.dot(op1_ref[...], w_ref[:, cols], preferred_element_type=F32) + inj_ref[:, cols].astype(F32)
        final_ref[:, cols] = jnp.where(deep, s2, s1_ref[:, cols]).astype(BF)
        back = nt(db_ref[...], w_ref[cols, :])
        part2 = jnp.sum(back * n0_ref[:, cols], axis=0, keepdims=True)
        part_ref[:, cols] += jnp.where(deep, part2, jnp.zeros_like(part2))
        return carry

    lax.fori_loop(0, 2, fourth, 0)


def core_call(place, op0, cb, n0, inj, cot, gain, pieces):
    vm = pl.BlockSpec(memory_space=pltpu.VMEM)
    return pl.pallas_call(
        core_kernel,
        out_shape=(
            jax.ShapeDtypeStruct((TOK, WP), BF),
            jax.ShapeDtypeStruct((TOK, WP), BF),
            jax.ShapeDtypeStruct((1, WP), F32),
        ),
        in_specs=[pl.BlockSpec(memory_space=pltpu.SMEM)] + [vm] * 6 + [pl.BlockSpec(memory_space=pl.ANY)] * 16,
        out_specs=(vm, vm, vm),
        scratch_shapes=[
            pltpu.VMEM((WP, WP), BF),
            pltpu.VMEM((TOK, WP), F32),
            pltpu.VMEM((TOK, WP), F32),
            pltpu.VMEM((TOK, WP), BF),
            pltpu.VMEM((TOK, WP), BF),
            pltpu.SemaphoreType.DMA((32,)),
        ],
        compiler_params=pltpu.CompilerParams(vmem_limit_bytes=48 * 2**20),
        cost_estimate=pl.CostEstimate(flops=8 * TOK * WP * WP, bytes_accessed=2 * WP * WP, transcendentals=0),
    )(place, op0, cb, n0, inj, cot, gain, *pieces)


def narrow(array):
    return array.T.reshape(16, SP, -1)[:, :SH].reshape(W, -1).T


def gather(own, acts):
    m1 = send(own, along(True, 1))
    m3 = send(own, along(True, -1))
    m2 = send(own, along(True, 2))
    three = jnp.stack([own, m1, m3])
    three1 = send(three, along(False, 1))
    three3 = send(three, along(False, -1))
    three1, three3, m2 = lax.optimization_barrier((three1, three3, m2))
    three2 = send(three1, along(False, 1))
    one3 = send(m2, along(False, -1))
    one1 = send(m2, along(False, 1))
    own4 = lax.optimization_barrier((three, m2, three1, three3, one3))
    one2 = send(own4[4], along(False, -1))
    early = tuple(send(a, SWAP) for a in own4)
    acts, early, (three2, one1, one2) = lax.optimization_barrier((acts, early, (three2, one1, one2)))
    late = tuple(send(a, SWAP) for a in (three2, one1, one2))
    mine = (three, m2, three1, one1, three2, one2, three3, one3)
    theirs = (early[0], early[1], early[2], late[1], late[0], late[2], early[3], early[4])
    return acts, mine + theirs


def total(part):
    dp_groups = [[yh * 16 + z * 2 + c for z in range(8) for c in range(2)] for yh in range(2)]
    got = lax.all_to_all(jnp.broadcast_to(part, (16, WP)), "dp", 0, 0, axis_index_groups=dp_groups)
    part = jnp.sum(got.reshape(16, WP), axis=0, keepdims=True)
    planes = [[line(x, y, z, c) for y in range(NY) for x in range(NX)] for z in range(NZ) for c in range(NC)]
    got = lax.all_to_all(jnp.broadcast_to(part, (32, WP)), AXES, 0, 0, axis_index_groups=planes)
    return jnp.sum(got.reshape(32, WP), axis=0, keepdims=True)


def shards(state0, injected, core_weight, gain, counts, cotangent):
    dp, fs = lax.axis_index("dp"), lax.axis_index("fsdp")
    pc = dp % 2
    place = jnp.stack([fs % 4, fs // 4, pc, counts[0]]).astype(jnp.int32)
    gain_w = jnp.pad(gain.reshape(16, SH), ((0, 0), (0, SP - SH))).reshape(1, WP)
    acts = prepare(state0, injected, cotangent, gain_w)
    (n0, op0, inj, cot, cb), pieces = gather(spread(place, core_weight), acts)
    final, injg, part = core_call(place, op0, cb, n0, inj, cot, gain_w, pieces)
    return (narrow(final), narrow(injg), narrow(total(part)).reshape(W))


def solution(mesh):
    rows = P(AXES, None)
    return jax.shard_map(
        shards,
        mesh=mesh,
        in_specs=(rows, rows, P("fsdp", None), P(), P(AXES), rows),
        out_specs=(rows, rows, P()),
        check_vma=False,
    )
```

```python
import itertools

import jax
import jax.numpy as jnp
from jax import lax
from jax.experimental import pallas as pl
from jax.experimental.pallas import tpu as pltpu
from jax.sharding import PartitionSpec as P

AXES = ("dp", "fsdp")
NX, NY, NZ, NC = 4, 8, 8, 2
YL = 4
W = 2640
SH = 165
SP = 176
WP = 16 * SP
HALF = WP // 2
TOK = 128
TILE = 256
EPS = 1e-06
BF = jnp.bfloat16
F32 = jnp.float32


def line(x, y, z, c):
    x, y, z, c = x % NX, y % NY, z % NZ, c % NC
    return ((y // YL) * NZ * NC + z * NC + c) * 16 + (y % YL) * NX + x


def chips():
    return itertools.product(range(NX), range(NY), range(NZ), range(NC))


def along(first, step):
    pairs = []
    for x, y, z, c in chips():
        in_x = (c == 0) == first
        pairs.append((line(x, y, z, c), line(x + step * in_x, y + step * (not in_x), z, c)))
    return pairs


SWAP = [(line(x, y, z, c), line(x, y, z, 1 - c)) for x, y, z, c in chips()]


def send(array, pairs):
    return lax.ppermute(array, AXES, pairs)


def nt(a, b):
    return lax.dot_general(a, b, (((1,), (1,)), ((), ())), preferred_element_type=F32)


def spread_kernel(place, w_ref, out_ref, wide_ref):
    wide_ref[...] = jnp.zeros_like(wide_ref)
    for t in range(20):
        wide_ref[0:SH, 128 * t : 128 * t + 128] = w_ref[:, 128 * t : 128 * t + 128].astype(F32)
    wide_ref[0:SH, 2560:W] = w_ref[:, 2560:W].astype(F32)
    lane = lax.broadcasted_iota(jnp.int32, (SP, 128), 1)
    for core in range(2):

        @pl.when(place[2] == core)
        def _():
            for t in range(HALF // 128):
                tile = jnp.zeros((SP, 128), F32)
                for j in range(8):
                    low, high = SP * j - 128 * t, SP * j + SH - 128 * t
                    if high <= 0 or low >= 128:
                        continue
                    q = SH * (8 * core + j) - low
                    base = (q // 128) * 128
                    win = wide_ref[:, base : base + 256]
                    moved = pltpu.roll(win, (base - q) % 256, 1)[:, :128]
                    tile = jnp.where((lane >= low) & (lane < high), moved, tile)
                out_ref[:, 128 * t : 128 * t + 128] = tile.astype(BF)

def spread(place, w):
    vm = pl.BlockSpec(memory_space=pltpu.VMEM)
    return pl.pallas_call(
        spread_kernel,
        out_shape=jax.ShapeDtypeStruct((SP, HALF), BF),
        in_specs=[pl.BlockSpec(memory_space=pltpu.SMEM), vm],
        out_specs=vm,
        scratch_shapes=[pltpu.VMEM((SP, 2944), F32)],
        compiler_params=pltpu.CompilerParams(vmem_limit_bytes=16 * 2**20),
    )(place, w)

def prepare_kernel(state_ref, inj_ref, cot_ref, gain_ref, n0_ref, op0_ref, injw_ref, cotw_ref, cb_ref, wide_ref, tall_ref):
    def regroup(src_ref):
        for s in range(16):
            wide_ref[SP * s : SP * s + SH, :] = src_ref[SH * s : SH * s + SH, :]

    for s in range(16):
        wide_ref[SP * s + SH : SP * s + SP, :] = jnp.zeros((SP - SH, TOK), F32)
    regroup(state_ref)
    acc = jnp.zeros((TOK, 128), F32)
    for t in range(WP // 128):
        cols = slice(128 * t, 128 * t + 128)
        s = wide_ref[cols, :].T
        n0_ref[:, cols] = s
        acc = acc + s * s
    inv = lax.rsqrt(jnp.sum(acc, axis=1, keepdims=True) / W + EPS)
    for t in range(WP // 128):
        cols = slice(128 * t, 128 * t + 128)
        n0 = n0_ref[:, cols] * inv
        n0_ref[:, cols] = n0
        op0_ref[:, cols] = (n0 * gain_ref[:, cols]).astype(BF)
    regroup(cot_ref)
    for t in range(WP // 128):
        cols = slice(128 * t, 128 * t + 128)
        c = wide_ref[cols, :].T
        cotw_ref[:, cols] = c
        cb_ref[:, cols] = c.astype(BF)
    tall_ref[...] = inj_ref[...].astype(F32)
    regroup(tall_ref)
    for t in range(WP // 128):
        cols = slice(128 * t, 128 * t + 128)
        injw_ref[:, cols] = wide_ref[cols, :].T.astype(BF)

def prepare(state, inj, cot, gain):
    vm = pl.BlockSpec(memory_space=pltpu.VMEM)
    wide = lambda dt: jax.ShapeDtypeStruct((TOK, WP), dt)
    return pl.pallas_call(
        prepare_kernel,
        out_shape=(wide(F32), wide(BF), wide(BF), wide(F32), wide(BF)),
        in_specs=[vm] * 4,
        out_specs=(vm,) * 5,
        scratch_shapes=[pltpu.VMEM((WP, TOK), F32), pltpu.VMEM((W, TOK), F32)],
        compiler_params=pltpu.CompilerParams(vmem_limit_bytes=24 * 2**20),
        cost_estimate=pl.CostEstimate(flops=10**6, bytes_accessed=10**7, transcendentals=0),
    )(state.T, inj.T, cot.T, gain)


PLACE = (0, 2, 6, 4)


def core_kernel(place, op0_ref, cb_ref, n0_ref, inj_ref, cot_ref, gain_ref, *rest):
    pieces = rest[:16]
    final_ref, injg_ref, part_ref = rest[16:19]
    w_ref, s1_ref, back_ref, op1_ref, db_ref, sems = rest[19:]
    px, py, pc, rounds = place[0], place[1], place[2], place[3]
    copies = []
    for who in range(2):
        core = pc if who == 0 else 1 - pc
        for k in range(4):
            for j in range(4):
                sx = jnp.where(core == 0, px + 4 - j, px + 4 - k) % 4
                sy = jnp.where(core == 0, py + 4 - k, py + 4 - j) % 4
                row = pl.multiple_of((sy * 4 + sx) * SP, SP)
                src = pieces[8 * who + PLACE[k] + j // 2].at[j % 2]
                dst = w_ref.at[pl.ds(row, SP), pl.ds(pl.multiple_of(core * HALF, 128), HALF)]
                copies.append(pltpu.make_async_copy(src, dst, sems.at[len(copies)]))
    for c in copies:
        c.start()
    deep = rounds >= 2

    ssq = jnp.zeros((TOK, 1), F32)
    for who in range(2):
        for c in copies[16 * who : 16 * who + 16]:
            c.wait()
        core = pc if who == 0 else 1 - pc
        cols = pl.ds(pl.multiple_of(core * HALF, 128), HALF)
        s1 = jnp.dot(op0_ref[...], w_ref[:, cols], preferred_element_type=F32) + inj_ref[:, cols].astype(F32)
        s1_ref[:, cols] = s1
        ssq = ssq + jnp.sum(s1 * s1, axis=1, keepdims=True)
        for t in range(2):
            rows = slice(t * HALF, t * HALF + HALF)
            back = nt(cb_ref[:, cols], w_ref[rows, cols])
            back_ref[:, rows] = back if who == 0 else back_ref[:, rows] + back
    inv1 = lax.rsqrt(ssq / W + EPS)

    def second(t, dots):
        cols = pl.ds(pl.multiple_of(t * TILE, TILE), TILE)
        n1 = s1_ref[:, cols] * inv1
        back = back_ref[:, cols]
        gain = gain_ref[:, cols]
        op1_ref[:, cols] = (n1 * gain).astype(BF)
        v = jnp.where(deep, n1, n0_ref[:, cols])
        part_ref[:, cols] = jnp.sum(back * v, axis=0, keepdims=True)
        return dots + jnp.sum(back * gain * n1, axis=1, keepdims=True)

    dots = lax.fori_loop(0, WP // TILE, second, jnp.zeros((TOK, 1), F32))
    mean1 = dots / W

    def third(t, carry):
        cols = pl.ds(pl.multiple_of(t * TILE, TILE), TILE)
        n1 = s1_ref[:, cols] * inv1
        d1 = inv1 * (back_ref[:, cols] * gain_ref[:, cols] - n1 * mean1)
        db_ref[:, cols] = d1.astype(BF)
        cot = cot_ref[:, cols]
        injg_ref[:, cols] = jnp.where(deep, cot + d1, cot).astype(BF)
        return carry

    lax.fori_loop(0, WP // TILE, third, 0)

    def fourth(t, carry):
        cols = pl.ds(pl.multiple_of(t * HALF, 128), HALF)
        s2 = jnp.dot(op1_ref[...], w_ref[:, cols], preferred_element_type=F32) + inj_ref[:, cols].astype(F32)
        final_ref[:, cols] = jnp.where(deep, s2, s1_ref[:, cols]).astype(BF)
        back = nt(db_ref[...], w_ref[cols, :])
        part2 = jnp.sum(back * n0_ref[:, cols], axis=0, keepdims=True)
        part_ref[:, cols] += jnp.where(deep, part2, jnp.zeros_like(part2))
        return carry

    lax.fori_loop(0, 2, fourth, 0)


def core_call(place, op0, cb, n0, inj, cot, gain, pieces):
    vm = pl.BlockSpec(memory_space=pltpu.VMEM)
    return pl.pallas_call(
        core_kernel,
        out_shape=(
            jax.ShapeDtypeStruct((TOK, WP), BF),
            jax.ShapeDtypeStruct((TOK, WP), BF),
            jax.ShapeDtypeStruct((1, WP), F32),
        ),
        in_specs=[pl.BlockSpec(memory_space=pltpu.SMEM)] + [vm] * 6 + [pl.BlockSpec(memory_space=pl.ANY)] * 16,
        out_specs=(vm, vm, vm),
        scratch_shapes=[
            pltpu.VMEM((WP, WP), BF),
            pltpu.VMEM((TOK, WP), F32),
            pltpu.VMEM((TOK, WP), F32),
            pltpu.VMEM((TOK, WP), BF),
            pltpu.VMEM((TOK, WP), BF),
            pltpu.SemaphoreType.DMA((32,)),
        ],
        compiler_params=pltpu.CompilerParams(vmem_limit_bytes=48 * 2**20),
        cost_estimate=pl.CostEstimate(flops=8 * TOK * WP * WP, bytes_accessed=2 * WP * WP, transcendentals=0),
    )(place, op0, cb, n0, inj, cot, gain, *pieces)


def narrow(array):
    return array.T.reshape(16, SP, -1)[:, :SH].reshape(W, -1).T


def gather(own, acts):
    down = send(own, along(True, -1))
    up = send(own, along(True, 1))
    far = send(own, along(True, 2))
    acts, down, up, far = lax.optimization_barrier((acts, down, up, far))
    low = jnp.stack([own, up])
    high = jnp.stack([far, down])
    near = (low, high)
    swapped = tuple(send(a, SWAP) for a in near)
    low3 = send(low, along(False, -1))
    high1 = send(high, along(False, 1))
    high3 = send(high, along(False, -1))
    low1 = send(low, along(False, 1))
    swapped, low3, high1, low1, high3 = lax.optimization_barrier((swapped, low3, high1, low1, high3))
    middle = (low1, high1, low3, high3)
    swapped += tuple(send(a, SWAP) for a in middle)
    high2 = send(high3, along(False, -1))
    low2 = send(low1, along(False, 1))
    swapped, low2, high2 = lax.optimization_barrier((swapped, low2, high2))
    last = (low2, high2)
    swapped += tuple(send(a, SWAP) for a in last)
    return acts, near + middle + last + swapped


def total(part):
    dp_groups = [[yh * 16 + z * 2 + c for z in range(8) for c in range(2)] for yh in range(2)]
    got = lax.all_to_all(jnp.broadcast_to(part, (16, WP)), "dp", 0, 0, axis_index_groups=dp_groups)
    part = jnp.sum(got.reshape(16, WP), axis=0, keepdims=True)
    planes = [[line(x, y, z, c) for y in range(NY) for x in range(NX)] for z in range(NZ) for c in range(NC)]
    got = lax.all_to_all(jnp.broadcast_to(part, (32, WP)), AXES, 0, 0, axis_index_groups=planes)
    return jnp.sum(got.reshape(32, WP), axis=0, keepdims=True)


def shards(state0, injected, core_weight, gain, counts, cotangent):
    dp, fs = lax.axis_index("dp"), lax.axis_index("fsdp")
    pc = dp % 2
    place = jnp.stack([fs % 4, fs // 4, pc, counts[0]]).astype(jnp.int32)
    gain_w = jnp.pad(gain.reshape(16, SH), ((0, 0), (0, SP - SH))).reshape(1, WP)
    acts = prepare(state0, injected, cotangent, gain_w)
    (n0, op0, inj, cot, cb), pieces = gather(spread(place, core_weight), acts)
    final, injg, part = core_call(place, op0, cb, n0, inj, cot, gain_w, pieces)
    return (narrow(final), narrow(injg), narrow(total(part)).reshape(W))


def solution(mesh):
    rows = P(AXES, None)
    return jax.shard_map(
        shards,
        mesh=mesh,
        in_specs=(rows, rows, P("fsdp", None), P(), P(AXES), rows),
        out_specs=(rows, rows, P()),
        check_vma=False,
    )
```

```python
import itertools

import jax
import jax.numpy as jnp
from jax import lax
from jax.experimental import pallas as pl
from jax.experimental.pallas import tpu as pltpu
from jax.sharding import PartitionSpec as P

AXES = ("dp", "fsdp")
NX, NY, NZ, NC = 4, 8, 8, 2
YL = 4
W = 2640
SH = 165
SP = 176
WP = 16 * SP
HALF = WP // 2
TOK = 128
TILE = 256
EPS = 1e-06
BF = jnp.bfloat16
F32 = jnp.float32


def line(x, y, z, c):
    x, y, z, c = x % NX, y % NY, z % NZ, c % NC
    return ((y // YL) * NZ * NC + z * NC + c) * 16 + (y % YL) * NX + x


def chips():
    return itertools.product(range(NX), range(NY), range(NZ), range(NC))


def along(first, step):
    pairs = []
    for x, y, z, c in chips():
        in_x = (c == 0) == first
        pairs.append((line(x, y, z, c), line(x + step * in_x, y + step * (not in_x), z, c)))
    return pairs


SWAP = [(line(x, y, z, c), line(x, y, z, 1 - c)) for x, y, z, c in chips()]


def send(array, pairs):
    return lax.ppermute(array, AXES, pairs)


def nt(a, b):
    return lax.dot_general(a, b, (((1,), (1,)), ((), ())), preferred_element_type=F32)


def spread_kernel(place, w_ref, out_ref, wide_ref):
    wide_ref[...] = jnp.zeros_like(wide_ref)
    for t in range(20):
        wide_ref[0:SH, 128 * t : 128 * t + 128] = w_ref[:, 128 * t : 128 * t + 128].astype(F32)
    wide_ref[0:SH, 2560:W] = w_ref[:, 2560:W].astype(F32)
    lane = lax.broadcasted_iota(jnp.int32, (SP, 128), 1)
    for core in range(2):

        @pl.when(place[2] == core)
        def _():
            for t in range(HALF // 128):
                tile = jnp.zeros((SP, 128), F32)
                for j in range(8):
                    low, high = SP * j - 128 * t, SP * j + SH - 128 * t
                    if high <= 0 or low >= 128:
                        continue
                    q = SH * (8 * core + j) - low
                    base = (q // 128) * 128
                    win = wide_ref[:, base : base + 256]
                    moved = pltpu.roll(win, (base - q) % 256, 1)[:, :128]
                    tile = jnp.where((lane >= low) & (lane < high), moved, tile)
                out_ref[:, 128 * t : 128 * t + 128] = tile.astype(BF)

def spread(place, w):
    vm = pl.BlockSpec(memory_space=pltpu.VMEM)
    return pl.pallas_call(
        spread_kernel,
        out_shape=jax.ShapeDtypeStruct((SP, HALF), BF),
        in_specs=[pl.BlockSpec(memory_space=pltpu.SMEM), vm],
        out_specs=vm,
        scratch_shapes=[pltpu.VMEM((SP, 2944), F32)],
        compiler_params=pltpu.CompilerParams(vmem_limit_bytes=16 * 2**20),
    )(place, w)

def prepare_kernel(state_ref, inj_ref, cot_ref, gain_ref, n0_ref, acts_ref, injw_ref, cotw_ref, wide_ref, tall_ref):
    def regroup(src_ref):
        for s in range(16):
            wide_ref[SP * s : SP * s + SH, :] = src_ref[SH * s : SH * s + SH, :]

    for s in range(16):
        wide_ref[SP * s + SH : SP * s + SP, :] = jnp.zeros((SP - SH, TOK), F32)
    regroup(state_ref)
    acc = jnp.zeros((TOK, 128), F32)
    for t in range(WP // 128):
        cols = slice(128 * t, 128 * t + 128)
        s = wide_ref[cols, :].T
        n0_ref[:, cols] = s
        acc = acc + s * s
    inv = lax.rsqrt(jnp.sum(acc, axis=1, keepdims=True) / W + EPS)
    for t in range(WP // 128):
        cols = slice(128 * t, 128 * t + 128)
        n0 = n0_ref[:, cols] * inv
        n0_ref[:, cols] = n0
        acts_ref[0, :, cols] = (n0 * gain_ref[:, cols]).astype(BF)
    regroup(cot_ref)
    for t in range(WP // 128):
        cols = slice(128 * t, 128 * t + 128)
        c = wide_ref[cols, :].T
        cotw_ref[:, cols] = c
        acts_ref[1, :, cols] = c.astype(BF)
    tall_ref[...] = inj_ref[...].astype(F32)
    regroup(tall_ref)
    for t in range(WP // 128):
        cols = slice(128 * t, 128 * t + 128)
        injw_ref[:, cols] = wide_ref[cols, :].T.astype(BF)

def prepare(state, inj, cot, gain):
    vm = pl.BlockSpec(memory_space=pltpu.VMEM)
    wide = lambda dt: jax.ShapeDtypeStruct((TOK, WP), dt)
    return pl.pallas_call(
        prepare_kernel,
        out_shape=(wide(F32), jax.ShapeDtypeStruct((2, TOK, WP), BF), wide(BF), wide(F32)),
        in_specs=[vm] * 4,
        out_specs=(vm,) * 4,
        scratch_shapes=[pltpu.VMEM((WP, TOK), F32), pltpu.VMEM((W, TOK), F32)],
        compiler_params=pltpu.CompilerParams(vmem_limit_bytes=24 * 2**20),
        cost_estimate=pl.CostEstimate(flops=10**6, bytes_accessed=10**7, transcendentals=0),
    )(state.T, inj.T, cot.T, gain)


PLACE = (0, 2, 6, 4)
ALL = 2 * TOK


def half_of(core):
    return pl.ds(pl.multiple_of(core * HALF, 128), HALF)


def first_kernel(place, acts_ref, peer_ref, *rest):
    pieces = rest[:8]
    s_ref, back_ref, give_ref, w_ref, both_ref, sems = rest[8:]
    px, py, pc = place[0], place[1], place[2]
    copies = []
    for k in range(4):
        for j in range(4):
            sx = jnp.where(pc == 0, px + 4 - j, px + 4 - k) % 4
            sy = jnp.where(pc == 0, py + 4 - k, py + 4 - j) % 4
            row = pl.multiple_of((sy * 4 + sx) * SP, SP)
            src = pieces[PLACE[k] + j // 2].at[j % 2]
            copies.append(pltpu.make_async_copy(src, w_ref.at[pl.ds(row, SP), :], sems.at[len(copies)]))
    for c in copies:
        c.start()
    both_ref[:TOK] = acts_ref[0]
    both_ref[TOK:] = peer_ref[0]
    grads = jnp.concatenate([acts_ref[1, :, half_of(pc)], peer_ref[1, :, half_of(pc)]], axis=0)
    for c in copies:
        c.wait()
    s1 = jnp.dot(both_ref[...], w_ref[...], preferred_element_type=F32)
    s_ref[...] = s1[:TOK]
    give_ref[:, :HALF] = s1[TOK:]
    for t in range(2):
        rows = slice(t * HALF, t * HALF + HALF)
        back = nt(grads, w_ref[rows, :])
        back_ref[:, rows] = back[:TOK]
        give_ref[:, HALF + t * HALF : 2 * HALF + t * HALF] = back[TOK:]


def middle_kernel(place, s_ref, back_ref, got_ref, n0_ref, inj_ref, cot_ref, gain_ref, next_ref, injg_ref, part_ref, s1_ref):
    pc, deep = place[2], place[3] >= 2
    mine, other = half_of(pc), half_of(1 - pc)
    s1_ref[:, mine] = s_ref[...] + inj_ref[:, mine].astype(F32)
    s1_ref[:, other] = got_ref[:, :HALF] + inj_ref[:, other].astype(F32)
    acc = jnp.zeros((TOK, 128), F32)
    for t in range(WP // 128):
        s1 = s1_ref[:, 128 * t : 128 * t + 128]
        acc = acc + s1 * s1
    inv1 = lax.rsqrt(jnp.sum(acc, axis=1, keepdims=True) / W + EPS)

    def second(t, acc):
        cols = pl.ds(pl.multiple_of(t * TILE, TILE), TILE)
        n1 = s1_ref[:, cols] * inv1
        back = back_ref[:, cols] + got_ref[:, pl.ds(pl.multiple_of(HALF + t * TILE, 128), TILE)]
        gain = gain_ref[:, cols]
        next_ref[0, :, cols] = (n1 * gain).astype(BF)
        part_ref[:, cols] = jnp.sum(back * jnp.where(deep, n1, n0_ref[:, cols]), axis=0, keepdims=True)
        return acc + back * gain * n1

    acc = lax.fori_loop(0, WP // TILE, second, jnp.zeros((TOK, TILE), F32))
    mean1 = jnp.sum(acc, axis=1, keepdims=True) / W

    def third(t, carry):
        cols = pl.ds(pl.multiple_of(t * TILE, TILE), TILE)
        n1 = s1_ref[:, cols] * inv1
        back = back_ref[:, cols] + got_ref[:, pl.ds(pl.multiple_of(HALF + t * TILE, 128), TILE)]
        d1 = jnp.where(deep, inv1 * (back * gain_ref[:, cols] - n1 * mean1), 0.0)
        next_ref[1, :, cols] = d1.astype(BF)
        injg_ref[:, cols] = (cot_ref[:, cols] + d1).astype(BF)
        return carry

    lax.fori_loop(0, WP // TILE, third, 0)


def last_kernel(place, next_ref, peer_ref, n0_ref, n0_peer_ref, part1_ref, w_ref, s_ref, give_ref, part_ref, both_ref):
    pc = place[2]
    grads = jnp.concatenate([next_ref[1, :, half_of(pc)], peer_ref[1, :, half_of(pc)]], axis=0)
    for t in range(2):
        rows = slice(t * HALF, t * HALF + HALF)
        back = nt(grads, w_ref[rows, :])
        sums = jnp.sum(back[:TOK] * n0_ref[:, rows] + back[TOK:] * n0_peer_ref[:, rows], axis=0, keepdims=True)
        part_ref[:, rows] = part1_ref[:, rows] + sums
    both_ref[:TOK] = next_ref[0]
    both_ref[TOK:] = peer_ref[0]
    s2 = jnp.dot(both_ref[...], w_ref[...], preferred_element_type=F32)
    s_ref[...] = s2[:TOK]
    give_ref[...] = s2[TOK:]


VM = pl.BlockSpec(memory_space=pltpu.VMEM)
SM = pl.BlockSpec(memory_space=pltpu.SMEM)
HB = pl.BlockSpec(memory_space=pl.ANY)


def shape(*dims, dtype=F32):
    return jax.ShapeDtypeStruct(dims, dtype)


def first_call(place, acts, peer, pieces):
    return pl.pallas_call(
        first_kernel,
        out_shape=(shape(TOK, HALF), shape(TOK, WP), shape(TOK, HALF + WP), shape(WP, HALF, dtype=BF)),
        in_specs=[SM, VM, VM] + [HB] * 8,
        out_specs=(VM,) * 4,
        scratch_shapes=[pltpu.VMEM((ALL, WP), BF), pltpu.SemaphoreType.DMA((16,))],
        compiler_params=pltpu.CompilerParams(vmem_limit_bytes=24 * 2**20),
        cost_estimate=pl.CostEstimate(flops=8 * TOK * WP * HALF, bytes_accessed=2 * WP * HALF, transcendentals=0),
    )(place, acts, peer, *pieces)


def middle_call(place, s_own, back, got, n0, inj, cot, gain):
    return pl.pallas_call(
        middle_kernel,
        out_shape=(shape(2, TOK, WP, dtype=BF), shape(TOK, WP, dtype=BF), shape(1, WP), shape(TOK, WP)),
        in_specs=[SM] + [VM] * 7,
        out_specs=(VM,) * 4,
        compiler_params=pltpu.CompilerParams(vmem_limit_bytes=20 * 2**20),
        cost_estimate=pl.CostEstimate(flops=20 * TOK * WP, bytes_accessed=10**7, transcendentals=0),
    )(place, s_own, back, got, n0, inj, cot, gain)


def last_call(place, nexts, peer, n0, n0_peer, part1, w):
    return pl.pallas_call(
        last_kernel,
        out_shape=(shape(TOK, HALF), shape(TOK, HALF), shape(1, WP)),
        in_specs=[SM] + [VM] * 6,
        out_specs=(VM,) * 3,
        scratch_shapes=[pltpu.VMEM((ALL, WP), BF)],
        compiler_params=pltpu.CompilerParams(vmem_limit_bytes=24 * 2**20),
        cost_estimate=pl.CostEstimate(flops=8 * TOK * WP * HALF, bytes_accessed=2 * WP * HALF, transcendentals=0),
    )(place, nexts, peer, n0, n0_peer, part1, w)


def narrow(array):
    return array.T.reshape(16, SP, -1)[:, :SH].reshape(W, -1).T


def gather(own, acts):
    down = send(own, along(True, -1))
    up = send(own, along(True, 1))
    far = send(own, along(True, 2))
    acts, down, up, far = lax.optimization_barrier((acts, down, up, far))
    low = jnp.stack([own, up])
    high = jnp.stack([far, down])
    low3 = send(low, along(False, -1))
    high1 = send(high, along(False, 1))
    high3 = send(high, along(False, -1))
    low1 = send(low, along(False, 1))
    high2 = send(high3, along(False, -1))
    low2 = send(low1, along(False, 1))
    return acts, (low, high, low1, high1, low3, high3, low2, high2)


def total(part):
    dp_groups = [[yh * 16 + z * 2 + c for z in range(8) for c in range(2)] for yh in range(2)]
    got = lax.all_to_all(jnp.broadcast_to(part, (16, WP)), "dp", 0, 0, axis_index_groups=dp_groups)
    part = jnp.sum(got.reshape(16, WP), axis=0, keepdims=True)
    planes = [[line(x, y, z, c) for y in range(NY) for x in range(NX)] for z in range(NZ) for c in range(NC)]
    got = lax.all_to_all(jnp.broadcast_to(part, (32, WP)), AXES, 0, 0, axis_index_groups=planes)
    return jnp.sum(got.reshape(32, WP), axis=0, keepdims=True)


def shards(state0, injected, core_weight, gain, counts, cotangent):
    dp, fs = lax.axis_index("dp"), lax.axis_index("fsdp")
    pc = dp % 2
    place = jnp.stack([fs % 4, fs // 4, pc, counts[0]]).astype(jnp.int32)
    gain_w = jnp.pad(gain.reshape(16, SH), ((0, 0), (0, SP - SH))).reshape(1, WP)
    acts = prepare(state0, injected, cotangent, gain_w)
    (n0, acts, inj, cot), pieces = gather(spread(place, core_weight), acts)
    peer, n0_peer = lax.optimization_barrier((send(acts, SWAP), send(n0, SWAP)))
    s_own, back, give, half = first_call(place, acts, peer, pieces)
    nexts, injg, part1, s1 = middle_call(place, s_own, back, send(give, SWAP), n0, inj, cot, gain_w)
    s_own, give, part = last_call(place, nexts, send(nexts, SWAP), n0, n0_peer, part1, half)
    got = send(give, SWAP)
    s2 = jnp.where(pc == 0, jnp.concatenate([s_own, got], axis=1), jnp.concatenate([got, s_own], axis=1))
    final = jnp.where(counts[0] >= 2, s2 + inj.astype(F32), s1).astype(BF)
    return (narrow(final), narrow(injg), narrow(total(part)).reshape(W))


def solution(mesh):
    rows = P(AXES, None)
    return jax.shard_map(
        shards,
        mesh=mesh,
        in_specs=(rows, rows, P("fsdp", None), P(), P(AXES), rows),
        out_specs=(rows, rows, P()),
        check_vma=False,
    )
```

```python
import itertools

import jax
import jax.numpy as jnp
from jax import lax
from jax.experimental import pallas as pl
from jax.experimental.pallas import tpu as pltpu
from jax.sharding import PartitionSpec as P

AXES = ("dp", "fsdp")
NX, NY, NZ, NC = 4, 8, 8, 2
YL = 4
W = 2640
SH = 165
SP = 176
WP = 16 * SP
HALF = WP // 2
TOK = 128
TILE = 256
EPS = 1e-06
BF = jnp.bfloat16
F32 = jnp.float32


def line(x, y, z, c):
    x, y, z, c = x % NX, y % NY, z % NZ, c % NC
    return ((y // YL) * NZ * NC + z * NC + c) * 16 + (y % YL) * NX + x


def chips():
    return itertools.product(range(NX), range(NY), range(NZ), range(NC))


def along(first, step):
    pairs = []
    for x, y, z, c in chips():
        in_x = (c == 0) == first
        pairs.append((line(x, y, z, c), line(x + step * in_x, y + step * (not in_x), z, c)))
    return pairs


SWAP = [(line(x, y, z, c), line(x, y, z, 1 - c)) for x, y, z, c in chips()]


def send(array, pairs):
    return lax.ppermute(array, AXES, pairs)


def nt(a, b):
    return lax.dot_general(a, b, (((1,), (1,)), ((), ())), preferred_element_type=F32)


def spread_kernel(place, w_ref, out_ref, wide_ref):
    wide_ref[...] = jnp.zeros_like(wide_ref)
    for t in range(20):
        wide_ref[0:SH, 128 * t : 128 * t + 128] = w_ref[:, 128 * t : 128 * t + 128].astype(F32)
    wide_ref[0:SH, 2560:W] = w_ref[:, 2560:W].astype(F32)
    lane = lax.broadcasted_iota(jnp.int32, (SP, 128), 1)
    for core in range(2):

        @pl.when(place[2] == core)
        def _():
            for t in range(HALF // 128):
                tile = jnp.zeros((SP, 128), F32)
                for j in range(8):
                    low, high = SP * j - 128 * t, SP * j + SH - 128 * t
                    if high <= 0 or low >= 128:
                        continue
                    q = SH * (8 * core + j) - low
                    base = (q // 128) * 128
                    win = wide_ref[:, base : base + 256]
                    moved = pltpu.roll(win, (base - q) % 256, 1)[:, :128]
                    tile = jnp.where((lane >= low) & (lane < high), moved, tile)
                out_ref[:, 128 * t : 128 * t + 128] = tile.astype(BF)

def spread(place, w):
    vm = pl.BlockSpec(memory_space=pltpu.VMEM)
    return pl.pallas_call(
        spread_kernel,
        out_shape=jax.ShapeDtypeStruct((SP, HALF), BF),
        in_specs=[pl.BlockSpec(memory_space=pltpu.SMEM), vm],
        out_specs=vm,
        scratch_shapes=[pltpu.VMEM((SP, 2944), F32)],
        compiler_params=pltpu.CompilerParams(vmem_limit_bytes=16 * 2**20),
    )(place, w)

def prepare_kernel(state_ref, inj_ref, cot_ref, gain_ref, n0_ref, acts_ref, injw_ref, cotw_ref, wide_ref, tall_ref):
    def regroup(src_ref):
        for s in range(16):
            wide_ref[SP * s : SP * s + SH, :] = src_ref[SH * s : SH * s + SH, :]

    for s in range(16):
        wide_ref[SP * s + SH : SP * s + SP, :] = jnp.zeros((SP - SH, TOK), F32)
    regroup(state_ref)
    acc = jnp.zeros((TOK, 128), F32)
    for t in range(WP // 128):
        cols = slice(128 * t, 128 * t + 128)
        s = wide_ref[cols, :].T
        n0_ref[:, cols] = s
        acc = acc + s * s
    inv = lax.rsqrt(jnp.sum(acc, axis=1, keepdims=True) / W + EPS)
    for t in range(WP // 128):
        cols = slice(128 * t, 128 * t + 128)
        n0 = n0_ref[:, cols] * inv
        n0_ref[:, cols] = n0
        acts_ref[0, :, cols] = (n0 * gain_ref[:, cols]).astype(BF)
    regroup(cot_ref)
    for t in range(WP // 128):
        cols = slice(128 * t, 128 * t + 128)
        c = wide_ref[cols, :].T
        cotw_ref[:, cols] = c
        acts_ref[1, :, cols] = c.astype(BF)
    tall_ref[...] = inj_ref[...].astype(F32)
    regroup(tall_ref)
    for t in range(WP // 128):
        cols = slice(128 * t, 128 * t + 128)
        injw_ref[:, cols] = wide_ref[cols, :].T.astype(BF)

def prepare(state, inj, cot, gain):
    vm = pl.BlockSpec(memory_space=pltpu.VMEM)
    wide = lambda dt: jax.ShapeDtypeStruct((TOK, WP), dt)
    return pl.pallas_call(
        prepare_kernel,
        out_shape=(wide(F32), jax.ShapeDtypeStruct((2, TOK, WP), BF), wide(BF), wide(F32)),
        in_specs=[vm] * 4,
        out_specs=(vm,) * 4,
        scratch_shapes=[pltpu.VMEM((WP, TOK), F32), pltpu.VMEM((W, TOK), F32)],
        compiler_params=pltpu.CompilerParams(vmem_limit_bytes=24 * 2**20),
        cost_estimate=pl.CostEstimate(flops=10**6, bytes_accessed=10**7, transcendentals=0),
    )(state.T, inj.T, cot.T, gain)


PLACE = (0, 2, 6, 4)
ALL = 2 * TOK


def half_of(core):
    return pl.ds(pl.multiple_of(core * HALF, 128), HALF)


def first_kernel(place, acts_ref, peer_ref, *rest):
    pieces = rest[:8]
    s_ref, back_ref, give_ref, w_ref, both_ref, sems = rest[8:]
    px, py, pc = place[0], place[1], place[2]
    copies = []
    for k in range(4):
        for j in range(4):
            sx = jnp.where(pc == 0, px + 4 - j, px + 4 - k) % 4
            sy = jnp.where(pc == 0, py + 4 - k, py + 4 - j) % 4
            row = pl.multiple_of((sy * 4 + sx) * SP, SP)
            src = pieces[PLACE[k] + j // 2].at[j % 2]
            copies.append(pltpu.make_async_copy(src, w_ref.at[pl.ds(row, SP), :], sems.at[len(copies)]))
    for c in copies:
        c.start()
    both_ref[:TOK] = acts_ref[0]
    both_ref[TOK:] = peer_ref[0]
    grads = jnp.concatenate([acts_ref[1, :, half_of(pc)], peer_ref[1, :, half_of(pc)]], axis=0)
    for c in copies:
        c.wait()
    s1 = jnp.dot(both_ref[...], w_ref[...], preferred_element_type=F32)
    s_ref[...] = s1[:TOK]
    give_ref[:, :HALF] = s1[TOK:]
    for t in range(2):
        rows = slice(t * HALF, t * HALF + HALF)
        back = nt(grads, w_ref[rows, :])
        back_ref[:, rows] = back[:TOK]
        give_ref[:, HALF + t * HALF : 2 * HALF + t * HALF] = back[TOK:]


def middle_kernel(place, s_ref, back_ref, got_ref, n0_ref, inj_ref, cot_ref, gain_ref, next_ref, injg_ref, part_ref, s1_ref):
    pc, deep = place[2], place[3] >= 2
    mine, other = half_of(pc), half_of(1 - pc)
    s1_ref[:, mine] = s_ref[...] + inj_ref[:, mine].astype(F32)
    s1_ref[:, other] = got_ref[:, :HALF] + inj_ref[:, other].astype(F32)
    acc = jnp.zeros((TOK, 128), F32)
    for t in range(WP // 128):
        s1 = s1_ref[:, 128 * t : 128 * t + 128]
        acc = acc + s1 * s1
    inv1 = lax.rsqrt(jnp.sum(acc, axis=1, keepdims=True) / W + EPS)

    def second(t, acc):
        cols = pl.ds(pl.multiple_of(t * TILE, TILE), TILE)
        n1 = s1_ref[:, cols] * inv1
        back = back_ref[:, cols] + got_ref[:, pl.ds(pl.multiple_of(HALF + t * TILE, 128), TILE)]
        gain = gain_ref[:, cols]
        next_ref[0, :, cols] = (n1 * gain).astype(BF)
        part_ref[:, cols] = jnp.sum(back * jnp.where(deep, n1, n0_ref[:, cols]), axis=0, keepdims=True)
        return acc + back * gain * n1

    acc = lax.fori_loop(0, WP // TILE, second, jnp.zeros((TOK, TILE), F32))
    mean1 = jnp.sum(acc, axis=1, keepdims=True) / W

    def third(t, carry):
        cols = pl.ds(pl.multiple_of(t * TILE, TILE), TILE)
        n1 = s1_ref[:, cols] * inv1
        back = back_ref[:, cols] + got_ref[:, pl.ds(pl.multiple_of(HALF + t * TILE, 128), TILE)]
        d1 = jnp.where(deep, inv1 * (back * gain_ref[:, cols] - n1 * mean1), 0.0)
        next_ref[1, :, cols] = d1.astype(BF)
        injg_ref[:, cols] = (cot_ref[:, cols] + d1).astype(BF)
        return carry

    lax.fori_loop(0, WP // TILE, third, 0)


def grads_kernel(place, next_ref, peer_ref, n0_ref, n0_peer_ref, part1_ref, w_ref, part_ref):
    pc = place[2]
    grads = jnp.concatenate([next_ref[1, :, half_of(pc)], peer_ref[1, :, half_of(pc)]], axis=0)
    for t in range(2):
        rows = slice(t * HALF, t * HALF + HALF)
        back = nt(grads, w_ref[rows, :])
        sums = jnp.sum(back[:TOK] * n0_ref[:, rows] + back[TOK:] * n0_peer_ref[:, rows], axis=0, keepdims=True)
        part_ref[:, rows] = part1_ref[:, rows] + sums


def state_kernel(next_ref, peer_ref, w_ref, s_ref, give_ref, both_ref):
    both_ref[:TOK] = next_ref[0]
    both_ref[TOK:] = peer_ref[0]
    s2 = jnp.dot(both_ref[...], w_ref[...], preferred_element_type=F32)
    s_ref[...] = s2[:TOK]
    give_ref[...] = s2[TOK:]


VM = pl.BlockSpec(memory_space=pltpu.VMEM)
SM = pl.BlockSpec(memory_space=pltpu.SMEM)
HB = pl.BlockSpec(memory_space=pl.ANY)


def shape(*dims, dtype=F32):
    return jax.ShapeDtypeStruct(dims, dtype)


def first_call(place, acts, peer, pieces):
    return pl.pallas_call(
        first_kernel,
        out_shape=(shape(TOK, HALF), shape(TOK, WP), shape(TOK, HALF + WP), shape(WP, HALF, dtype=BF)),
        in_specs=[SM, VM, VM] + [HB] * 8,
        out_specs=(VM,) * 4,
        scratch_shapes=[pltpu.VMEM((ALL, WP), BF), pltpu.SemaphoreType.DMA((16,))],
        compiler_params=pltpu.CompilerParams(vmem_limit_bytes=24 * 2**20),
        cost_estimate=pl.CostEstimate(flops=8 * TOK * WP * HALF, bytes_accessed=2 * WP * HALF, transcendentals=0),
    )(place, acts, peer, *pieces)


def middle_call(place, s_own, back, got, n0, inj, cot, gain):
    return pl.pallas_call(
        middle_kernel,
        out_shape=(shape(2, TOK, WP, dtype=BF), shape(TOK, WP, dtype=BF), shape(1, WP), shape(TOK, WP)),
        in_specs=[SM] + [VM] * 7,
        out_specs=(VM,) * 4,
        compiler_params=pltpu.CompilerParams(vmem_limit_bytes=20 * 2**20),
        cost_estimate=pl.CostEstimate(flops=20 * TOK * WP, bytes_accessed=10**7, transcendentals=0),
    )(place, s_own, back, got, n0, inj, cot, gain)


def grads_call(place, nexts, peer, n0, n0_peer, part1, w):
    return pl.pallas_call(
        grads_kernel,
        out_shape=shape(1, WP),
        in_specs=[SM] + [VM] * 6,
        out_specs=VM,
        compiler_params=pltpu.CompilerParams(vmem_limit_bytes=24 * 2**20),
        cost_estimate=pl.CostEstimate(flops=4 * TOK * WP * HALF, bytes_accessed=2 * WP * HALF, transcendentals=0),
    )(place, nexts, peer, n0, n0_peer, part1, w)


def state_call(nexts, peer, w):
    return pl.pallas_call(
        state_kernel,
        out_shape=(shape(TOK, HALF), shape(TOK, HALF)),
        in_specs=[VM] * 3,
        out_specs=(VM,) * 2,
        scratch_shapes=[pltpu.VMEM((ALL, WP), BF)],
        compiler_params=pltpu.CompilerParams(vmem_limit_bytes=24 * 2**20),
        cost_estimate=pl.CostEstimate(flops=4 * TOK * WP * HALF, bytes_accessed=2 * WP * HALF, transcendentals=0),
    )(nexts, peer, w)


def narrow(array):
    return array.T.reshape(16, SP, -1)[:, :SH].reshape(W, -1).T


def gather(own, acts):
    down = send(own, along(True, -1))
    up = send(own, along(True, 1))
    far = send(own, along(True, 2))
    acts, down, up, far = lax.optimization_barrier((acts, down, up, far))
    low = jnp.stack([own, up])
    high = jnp.stack([far, down])
    low3 = send(low, along(False, -1))
    high1 = send(high, along(False, 1))
    high3 = send(high, along(False, -1))
    low1 = send(low, along(False, 1))
    high2 = send(high3, along(False, -1))
    low2 = send(low1, along(False, 1))
    high1, low3, acts = lax.optimization_barrier((high1, low3, acts))
    return acts, (low, high, low1, high1, low3, high3, low2, high2)


def groups(axis):
    found = {}
    for x, y, z, c in chips():
        key = {"z": (x, y, c), "y": (x, z, c), "xc": (y, z)}[axis]
        found.setdefault(key, []).append(line(x, y, z, c))
    return list(found.values())


def total(part, axis):
    got = lax.all_to_all(jnp.broadcast_to(part, (8, WP)), AXES, 0, 0, axis_index_groups=groups(axis))
    return jnp.sum(got.reshape(8, WP), axis=0, keepdims=True)


def shards(state0, injected, core_weight, gain, counts, cotangent):
    dp, fs = lax.axis_index("dp"), lax.axis_index("fsdp")
    pc = dp % 2
    place = jnp.stack([fs % 4, fs // 4, pc, counts[0]]).astype(jnp.int32)
    gain_w = jnp.pad(gain.reshape(16, SH), ((0, 0), (0, SP - SH))).reshape(1, WP)
    acts = prepare(state0, injected, cotangent, gain_w)
    (n0, acts, inj, cot), pieces = gather(spread(place, core_weight), acts)
    peer, n0_peer = lax.optimization_barrier((send(acts, SWAP), send(n0, SWAP)))
    s_own, back, give, half = first_call(place, acts, peer, pieces)
    nexts, injg, part1, s1 = middle_call(place, s_own, back, send(give, SWAP), n0, inj, cot, gain_w)
    peer = send(nexts, SWAP)
    part = grads_call(place, nexts, peer, n0, n0_peer, part1, half)
    part = total(part, "z")
    s_own, give = state_call(nexts, peer, half)
    got, s_own, part = lax.optimization_barrier((send(give, SWAP), s_own, part))
    part = total(part, "y")
    injg, part = lax.optimization_barrier((narrow(injg), part))
    part = total(part, "xc")
    s2 = jnp.where(pc == 0, jnp.concatenate([s_own, got], axis=1), jnp.concatenate([got, s_own], axis=1))
    final = jnp.where(counts[0] >= 2, s2 + inj.astype(F32), s1).astype(BF)
    return (narrow(final), injg, narrow(part).reshape(W))


def solution(mesh):
    rows = P(AXES, None)
    return jax.shard_map(
        shards,
        mesh=mesh,
        in_specs=(rows, rows, P("fsdp", None), P(), P(AXES), rows),
        out_specs=(rows, rows, P()),
        check_vma=False,
    )
```

```python
import itertools

import jax
import jax.numpy as jnp
from jax import lax
from jax.experimental import pallas as pl
from jax.experimental.pallas import tpu as pltpu
from jax.sharding import PartitionSpec as P

AXES = ("dp", "fsdp")
NX, NY, NZ, NC = 4, 8, 8, 2
YL = 4
W = 2640
SH = 165
SP = 176
WP = 16 * SP
HALF = WP // 2
TOK = 128
TILE = 256
EPS = 1e-06
BF = jnp.bfloat16
F32 = jnp.float32


def line(x, y, z, c):
    x, y, z, c = x % NX, y % NY, z % NZ, c % NC
    return ((y // YL) * NZ * NC + z * NC + c) * 16 + (y % YL) * NX + x


def chips():
    return itertools.product(range(NX), range(NY), range(NZ), range(NC))


def along(first, step):
    pairs = []
    for x, y, z, c in chips():
        in_x = (c == 0) == first
        pairs.append((line(x, y, z, c), line(x + step * in_x, y + step * (not in_x), z, c)))
    return pairs


SWAP = [(line(x, y, z, c), line(x, y, z, 1 - c)) for x, y, z, c in chips()]


def send(array, pairs):
    return lax.ppermute(array, AXES, pairs)


def nt(a, b):
    return lax.dot_general(a, b, (((1,), (1,)), ((), ())), preferred_element_type=F32)


def spread_kernel(place, w_ref, out_ref, wide_ref):
    wide_ref[...] = jnp.zeros_like(wide_ref)
    for t in range(20):
        wide_ref[0:SH, 128 * t : 128 * t + 128] = w_ref[:, 128 * t : 128 * t + 128].astype(F32)
    wide_ref[0:SH, 2560:W] = w_ref[:, 2560:W].astype(F32)
    lane = lax.broadcasted_iota(jnp.int32, (SP, 128), 1)
    for core in range(2):

        @pl.when(place[2] == core)
        def _():
            for t in range(HALF // 128):
                tile = jnp.zeros((SP, 128), F32)
                for j in range(8):
                    low, high = SP * j - 128 * t, SP * j + SH - 128 * t
                    if high <= 0 or low >= 128:
                        continue
                    q = SH * (8 * core + j) - low
                    base = (q // 128) * 128
                    win = wide_ref[:, base : base + 256]
                    moved = pltpu.roll(win, (base - q) % 256, 1)[:, :128]
                    tile = jnp.where((lane >= low) & (lane < high), moved, tile)
                out_ref[:, 128 * t : 128 * t + 128] = tile.astype(BF)

def spread(place, w):
    vm = pl.BlockSpec(memory_space=pltpu.VMEM)
    return pl.pallas_call(
        spread_kernel,
        out_shape=jax.ShapeDtypeStruct((SP, HALF), BF),
        in_specs=[pl.BlockSpec(memory_space=pltpu.SMEM), vm],
        out_specs=vm,
        scratch_shapes=[pltpu.VMEM((SP, 2944), F32)],
        compiler_params=pltpu.CompilerParams(vmem_limit_bytes=16 * 2**20),
    )(place, w)

def prepare_kernel(state_ref, inj_ref, cot_ref, gain_ref, n0_ref, acts_ref, injw_ref, cotw_ref, wide_ref, tall_ref):
    def regroup(src_ref):
        for s in range(16):
            wide_ref[SP * s : SP * s + SH, :] = src_ref[SH * s : SH * s + SH, :]

    for s in range(16):
        wide_ref[SP * s + SH : SP * s + SP, :] = jnp.zeros((SP - SH, TOK), F32)
    regroup(state_ref)
    acc = jnp.zeros((TOK, 128), F32)
    for t in range(WP // 128):
        cols = slice(128 * t, 128 * t + 128)
        s = wide_ref[cols, :].T
        n0_ref[:, cols] = s
        acc = acc + s * s
    inv = lax.rsqrt(jnp.sum(acc, axis=1, keepdims=True) / W + EPS)
    for t in range(WP // 128):
        cols = slice(128 * t, 128 * t + 128)
        n0 = n0_ref[:, cols] * inv
        n0_ref[:, cols] = n0
        acts_ref[0, :, cols] = (n0 * gain_ref[:, cols]).astype(BF)
    regroup(cot_ref)
    for t in range(WP // 128):
        cols = slice(128 * t, 128 * t + 128)
        c = wide_ref[cols, :].T
        cotw_ref[:, cols] = c
        acts_ref[1, :, cols] = c.astype(BF)
    tall_ref[...] = inj_ref[...].astype(F32)
    regroup(tall_ref)
    for t in range(WP // 128):
        cols = slice(128 * t, 128 * t + 128)
        injw_ref[:, cols] = wide_ref[cols, :].T.astype(BF)

def prepare(state, inj, cot, gain):
    vm = pl.BlockSpec(memory_space=pltpu.VMEM)
    wide = lambda dt: jax.ShapeDtypeStruct((TOK, WP), dt)
    return pl.pallas_call(
        prepare_kernel,
        out_shape=(wide(F32), jax.ShapeDtypeStruct((2, TOK, WP), BF), wide(BF), wide(F32)),
        in_specs=[vm] * 4,
        out_specs=(vm,) * 4,
        scratch_shapes=[pltpu.VMEM((WP, TOK), F32), pltpu.VMEM((W, TOK), F32)],
        compiler_params=pltpu.CompilerParams(vmem_limit_bytes=24 * 2**20),
        cost_estimate=pl.CostEstimate(flops=10**6, bytes_accessed=10**7, transcendentals=0),
    )(state.T, inj.T, cot.T, gain)


PLACE = (0, 2, 6, 4)
ALL = 2 * TOK


def half_of(core):
    return pl.ds(pl.multiple_of(core * HALF, 128), HALF)


def first_kernel(place, acts_ref, peer_ref, *rest):
    pieces = rest[:8]
    s_ref, back_ref, give_ref, w_ref, both_ref, sems = rest[8:]
    px, py, pc = place[0], place[1], place[2]
    copies = []
    for k in range(4):
        for j in range(4):
            sx = jnp.where(pc == 0, px + 4 - j, px + 4 - k) % 4
            sy = jnp.where(pc == 0, py + 4 - k, py + 4 - j) % 4
            row = pl.multiple_of((sy * 4 + sx) * SP, SP)
            src = pieces[PLACE[k] + j // 2].at[j % 2]
            copies.append(pltpu.make_async_copy(src, w_ref.at[pl.ds(row, SP), :], sems.at[len(copies)]))
    for c in copies:
        c.start()
    both_ref[:TOK] = acts_ref[0]
    both_ref[TOK:] = peer_ref[0]
    grads = jnp.concatenate([acts_ref[1, :, half_of(pc)], peer_ref[1, :, half_of(pc)]], axis=0)
    for c in copies:
        c.wait()
    s1 = jnp.dot(both_ref[...], w_ref[...], preferred_element_type=F32)
    s_ref[...] = s1[:TOK]
    give_ref[:, :HALF] = s1[TOK:]
    for t in range(2):
        rows = slice(t * HALF, t * HALF + HALF)
        back = nt(grads, w_ref[rows, :])
        back_ref[:, rows] = back[:TOK]
        give_ref[:, HALF + t * HALF : 2 * HALF + t * HALF] = back[TOK:]


def middle_kernel(place, s_ref, back_ref, got_ref, n0_ref, inj_ref, cot_ref, gain_ref, next_ref, injg_ref, part_ref, s1_ref):
    pc, deep = place[2], place[3] >= 2
    mine, other = half_of(pc), half_of(1 - pc)
    s1_ref[:, mine] = s_ref[...] + inj_ref[:, mine].astype(F32)
    s1_ref[:, other] = got_ref[:, :HALF] + inj_ref[:, other].astype(F32)
    acc = jnp.zeros((TOK, 128), F32)
    for t in range(WP // 128):
        s1 = s1_ref[:, 128 * t : 128 * t + 128]
        acc = acc + s1 * s1
    inv1 = lax.rsqrt(jnp.sum(acc, axis=1, keepdims=True) / W + EPS)

    def second(t, acc):
        cols = pl.ds(pl.multiple_of(t * TILE, TILE), TILE)
        n1 = s1_ref[:, cols] * inv1
        back = back_ref[:, cols] + got_ref[:, pl.ds(pl.multiple_of(HALF + t * TILE, 128), TILE)]
        gain = gain_ref[:, cols]
        next_ref[0, :, cols] = (n1 * gain).astype(BF)
        part_ref[:, cols] = jnp.sum(back * jnp.where(deep, n1, n0_ref[:, cols]), axis=0, keepdims=True)
        return acc + back * gain * n1

    acc = lax.fori_loop(0, WP // TILE, second, jnp.zeros((TOK, TILE), F32))
    mean1 = jnp.sum(acc, axis=1, keepdims=True) / W

    def third(t, carry):
        cols = pl.ds(pl.multiple_of(t * TILE, TILE), TILE)
        n1 = s1_ref[:, cols] * inv1
        back = back_ref[:, cols] + got_ref[:, pl.ds(pl.multiple_of(HALF + t * TILE, 128), TILE)]
        d1 = jnp.where(deep, inv1 * (back * gain_ref[:, cols] - n1 * mean1), 0.0)
        next_ref[1, :, cols] = d1.astype(BF)
        injg_ref[:, cols] = (cot_ref[:, cols] + d1).astype(BF)
        return carry

    lax.fori_loop(0, WP // TILE, third, 0)


def grads_kernel(place, next_ref, peer_ref, n0_ref, n0_peer_ref, part1_ref, w_ref, part_ref):
    pc = place[2]
    grads = jnp.concatenate([next_ref[1, :, half_of(pc)], peer_ref[1, :, half_of(pc)]], axis=0)
    for t in range(2):
        rows = slice(t * HALF, t * HALF + HALF)
        back = nt(grads, w_ref[rows, :])
        sums = jnp.sum(back[:TOK] * n0_ref[:, rows] + back[TOK:] * n0_peer_ref[:, rows], axis=0, keepdims=True)
        part_ref[:, rows] = part1_ref[:, rows] + sums


def state_kernel(next_ref, peer_ref, w_ref, s_ref, give_ref, both_ref):
    both_ref[:TOK] = next_ref[0]
    both_ref[TOK:] = peer_ref[0]
    s2 = jnp.dot(both_ref[...], w_ref[...], preferred_element_type=F32)
    s_ref[...] = s2[:TOK]
    give_ref[...] = s2[TOK:]


VM = pl.BlockSpec(memory_space=pltpu.VMEM)
SM = pl.BlockSpec(memory_space=pltpu.SMEM)
HB = pl.BlockSpec(memory_space=pl.ANY)


def shape(*dims, dtype=F32):
    return jax.ShapeDtypeStruct(dims, dtype)


def first_call(place, acts, peer, pieces):
    return pl.pallas_call(
        first_kernel,
        out_shape=(shape(TOK, HALF), shape(TOK, WP), shape(TOK, HALF + WP), shape(WP, HALF, dtype=BF)),
        in_specs=[SM, VM, VM] + [HB] * 8,
        out_specs=(VM,) * 4,
        scratch_shapes=[pltpu.VMEM((ALL, WP), BF), pltpu.SemaphoreType.DMA((16,))],
        compiler_params=pltpu.CompilerParams(vmem_limit_bytes=24 * 2**20),
        cost_estimate=pl.CostEstimate(flops=8 * TOK * WP * HALF, bytes_accessed=2 * WP * HALF, transcendentals=0),
    )(place, acts, peer, *pieces)


def middle_call(place, s_own, back, got, n0, inj, cot, gain):
    return pl.pallas_call(
        middle_kernel,
        out_shape=(shape(2, TOK, WP, dtype=BF), shape(TOK, WP, dtype=BF), shape(1, WP), shape(TOK, WP)),
        in_specs=[SM] + [VM] * 7,
        out_specs=(VM,) * 4,
        compiler_params=pltpu.CompilerParams(vmem_limit_bytes=20 * 2**20),
        cost_estimate=pl.CostEstimate(flops=20 * TOK * WP, bytes_accessed=10**7, transcendentals=0),
    )(place, s_own, back, got, n0, inj, cot, gain)


def grads_call(place, nexts, peer, n0, n0_peer, part1, w):
    return pl.pallas_call(
        grads_kernel,
        out_shape=shape(1, WP),
        in_specs=[SM] + [VM] * 6,
        out_specs=VM,
        compiler_params=pltpu.CompilerParams(vmem_limit_bytes=24 * 2**20),
        cost_estimate=pl.CostEstimate(flops=4 * TOK * WP * HALF, bytes_accessed=2 * WP * HALF, transcendentals=0),
    )(place, nexts, peer, n0, n0_peer, part1, w)


def state_call(nexts, peer, w):
    return pl.pallas_call(
        state_kernel,
        out_shape=(shape(TOK, HALF), shape(TOK, HALF)),
        in_specs=[VM] * 3,
        out_specs=(VM,) * 2,
        scratch_shapes=[pltpu.VMEM((ALL, WP), BF)],
        compiler_params=pltpu.CompilerParams(vmem_limit_bytes=24 * 2**20),
        cost_estimate=pl.CostEstimate(flops=4 * TOK * WP * HALF, bytes_accessed=2 * WP * HALF, transcendentals=0),
    )(nexts, peer, w)


def tighten(wide_ref, tall_ref, out_ref):
    for s in range(16):
        tall_ref[SH * s : SH * s + SH, :] = wide_ref[SP * s : SP * s + SH, :]
    out_ref[...] = tall_ref[...].astype(BF)


def flip_kernel(rows_ref, out_ref, wide_ref, tall_ref):
    for t in range(WP // 128):
        cols = slice(128 * t, 128 * t + 128)
        wide_ref[cols, :] = rows_ref[:, cols].astype(F32).T
    tighten(wide_ref, tall_ref, out_ref)


def final_kernel(place, s_ref, got_ref, inj_ref, s1_ref, out_ref, s2_ref, wide_ref, tall_ref):
    pc, deep = place[2], place[3] >= 2
    s2_ref[:, half_of(pc)] = s_ref[...]
    s2_ref[:, half_of(1 - pc)] = got_ref[...]
    for t in range(WP // 128):
        cols = slice(128 * t, 128 * t + 128)
        s2 = s2_ref[:, cols] + inj_ref[:, cols].astype(F32)
        wide_ref[cols, :] = jnp.where(deep, s2, s1_ref[:, cols]).T
    tighten(wide_ref, tall_ref, out_ref)


FLIPPED = [pltpu.VMEM((WP, TOK), F32), pltpu.VMEM((W, TOK), F32)]


def flip_call(rows):
    return pl.pallas_call(
        flip_kernel,
        out_shape=shape(W, TOK, dtype=BF),
        in_specs=[VM],
        out_specs=VM,
        scratch_shapes=FLIPPED,
        compiler_params=pltpu.CompilerParams(vmem_limit_bytes=16 * 2**20),
        cost_estimate=pl.CostEstimate(flops=10**6, bytes_accessed=3 * 10**6, transcendentals=0),
    )(rows).T


def final_call(place, s_own, got, inj, s1):
    return pl.pallas_call(
        final_kernel,
        out_shape=shape(W, TOK, dtype=BF),
        in_specs=[SM] + [VM] * 4,
        out_specs=VM,
        scratch_shapes=[pltpu.VMEM((TOK, WP), F32)] + FLIPPED,
        compiler_params=pltpu.CompilerParams(vmem_limit_bytes=16 * 2**20),
        cost_estimate=pl.CostEstimate(flops=10**6, bytes_accessed=5 * 10**6, transcendentals=0),
    )(place, s_own, got, inj, s1).T


def gather(own, acts):
    down = send(own, along(True, -1))
    up = send(own, along(True, 1))
    far = send(own, along(True, 2))
    acts, down, up, far = lax.optimization_barrier((acts, down, up, far))
    low = jnp.stack([own, up])
    high = jnp.stack([far, down])
    low3 = send(low, along(False, -1))
    high1 = send(high, along(False, 1))
    high3 = send(high, along(False, -1))
    low1 = send(low, along(False, 1))
    high2 = send(high3, along(False, -1))
    low2 = send(low1, along(False, 1))
    return acts, (low, high, low1, high1, low3, high3, low2, high2)


def groups(axis):
    found = {}
    for x, y, z, c in chips():
        key = {"z": (x, y, c), "y": (x, z, c), "xc": (y, z)}[axis]
        found.setdefault(key, []).append(line(x, y, z, c))
    return list(found.values())


def total(part, axis):
    got = lax.all_to_all(jnp.broadcast_to(part, (8, WP)), AXES, 0, 0, axis_index_groups=groups(axis))
    return jnp.sum(got.reshape(8, WP), axis=0, keepdims=True)


def shards(state0, injected, core_weight, gain, counts, cotangent):
    dp, fs = lax.axis_index("dp"), lax.axis_index("fsdp")
    pc = dp % 2
    place = jnp.stack([fs % 4, fs // 4, pc, counts[0]]).astype(jnp.int32)
    gain_w = jnp.pad(gain.reshape(16, SH), ((0, 0), (0, SP - SH))).reshape(1, WP)
    acts = prepare(state0, injected, cotangent, gain_w)
    (n0, acts, inj, cot), pieces = gather(spread(place, core_weight), acts)
    peer, n0 = lax.optimization_barrier((send(acts, SWAP), n0))
    peer, n0_peer = lax.optimization_barrier((peer, send(n0, SWAP)))
    s_own, back, give, half = first_call(place, acts, peer, pieces)
    nexts, injg, part1, s1 = middle_call(place, s_own, back, send(give, SWAP), n0, inj, cot, gain_w)
    peer = send(nexts, SWAP)
    part = grads_call(place, nexts, peer, n0, n0_peer, part1, half)
    part = total(part, "z")
    s_own, give = state_call(nexts, peer, half)
    got, s_own, part = lax.optimization_barrier((send(give, SWAP), s_own, part))
    part = total(part, "y")
    injg, part = lax.optimization_barrier((flip_call(injg), part))
    part = total(part, "xc")
    final = final_call(place, s_own, got, inj, s1)
    return (final, injg, part.reshape(16, SP)[:, :SH].reshape(W))


def solution(mesh):
    rows = P(AXES, None)
    return jax.shard_map(
        shards,
        mesh=mesh,
        in_specs=(rows, rows, P("fsdp", None), P(), P(AXES), rows),
        out_specs=(rows, rows, P()),
        check_vma=False,
    )
```

```python
import itertools

import jax
import jax.numpy as jnp
from jax import lax
from jax.experimental import pallas as pl
from jax.experimental.pallas import tpu as pltpu
from jax.sharding import PartitionSpec as P

AXES = ("dp", "fsdp")
NX, NY, NZ, NC = 4, 8, 8, 2
YL = 4
W = 2640
SH = 165
SP = 176
WP = 16 * SP
HALF = WP // 2
TOK = 128
TILE = 256
EPS = 1e-06
BF = jnp.bfloat16
F32 = jnp.float32


def line(x, y, z, c):
    x, y, z, c = x % NX, y % NY, z % NZ, c % NC
    return ((y // YL) * NZ * NC + z * NC + c) * 16 + (y % YL) * NX + x


def chips():
    return itertools.product(range(NX), range(NY), range(NZ), range(NC))


def along(first, step):
    pairs = []
    for x, y, z, c in chips():
        in_x = (c == 0) == first
        pairs.append((line(x, y, z, c), line(x + step * in_x, y + step * (not in_x), z, c)))
    return pairs


SWAP = [(line(x, y, z, c), line(x, y, z, 1 - c)) for x, y, z, c in chips()]


def send(array, pairs):
    return lax.ppermute(array, AXES, pairs)


def nt(a, b):
    return lax.dot_general(a, b, (((1,), (1,)), ((), ())), preferred_element_type=F32)


def spread_kernel(place, w_ref, out_ref, wide_ref):
    wide_ref[...] = jnp.zeros_like(wide_ref)
    for t in range(20):
        wide_ref[0:SH, 128 * t : 128 * t + 128] = w_ref[:, 128 * t : 128 * t + 128].astype(F32)
    wide_ref[0:SH, 2560:W] = w_ref[:, 2560:W].astype(F32)
    lane = lax.broadcasted_iota(jnp.int32, (SP, 128), 1)
    for core in range(2):

        @pl.when(place[2] == core)
        def _():
            for t in range(HALF // 128):
                tile = jnp.zeros((SP, 128), F32)
                for j in range(8):
                    low, high = SP * j - 128 * t, SP * j + SH - 128 * t
                    if high <= 0 or low >= 128:
                        continue
                    q = SH * (8 * core + j) - low
                    base = (q // 128) * 128
                    win = wide_ref[:, base : base + 256]
                    moved = pltpu.roll(win, (base - q) % 256, 1)[:, :128]
                    tile = jnp.where((lane >= low) & (lane < high), moved, tile)
                out_ref[:, 128 * t : 128 * t + 128] = tile.astype(BF)

def spread(place, w):
    vm = pl.BlockSpec(memory_space=pltpu.VMEM)
    return pl.pallas_call(
        spread_kernel,
        out_shape=jax.ShapeDtypeStruct((SP, HALF), BF),
        in_specs=[pl.BlockSpec(memory_space=pltpu.SMEM), vm],
        out_specs=vm,
        scratch_shapes=[pltpu.VMEM((SP, 2944), F32)],
        compiler_params=pltpu.CompilerParams(vmem_limit_bytes=16 * 2**20),
    )(place, w)

def prepare_kernel(state_ref, inj_ref, cot_ref, gain_ref, n0_ref, acts_ref, injw_ref, cotw_ref, wide_ref, tall_ref):
    def regroup(src_ref):
        for s in range(16):
            wide_ref[SP * s : SP * s + SH, :] = src_ref[SH * s : SH * s + SH, :]

    for s in range(16):
        wide_ref[SP * s + SH : SP * s + SP, :] = jnp.zeros((SP - SH, TOK), F32)
    regroup(state_ref)
    acc = jnp.zeros((TOK, 128), F32)
    for t in range(WP // 128):
        cols = slice(128 * t, 128 * t + 128)
        s = wide_ref[cols, :].T
        n0_ref[:, cols] = s
        acc = acc + s * s
    inv = lax.rsqrt(jnp.sum(acc, axis=1, keepdims=True) / W + EPS)
    for t in range(WP // 128):
        cols = slice(128 * t, 128 * t + 128)
        n0 = n0_ref[:, cols] * inv
        n0_ref[:, cols] = n0
        acts_ref[0, :, cols] = (n0 * gain_ref[:, cols]).astype(BF)
    regroup(cot_ref)
    for t in range(WP // 128):
        cols = slice(128 * t, 128 * t + 128)
        c = wide_ref[cols, :].T
        cotw_ref[:, cols] = c
        acts_ref[1, :, cols] = c.astype(BF)
    tall_ref[...] = inj_ref[...].astype(F32)
    regroup(tall_ref)
    for t in range(WP // 128):
        cols = slice(128 * t, 128 * t + 128)
        injw_ref[:, cols] = wide_ref[cols, :].T.astype(BF)

def prepare(state, inj, cot, gain):
    vm = pl.BlockSpec(memory_space=pltpu.VMEM)
    wide = lambda dt: jax.ShapeDtypeStruct((TOK, WP), dt)
    return pl.pallas_call(
        prepare_kernel,
        out_shape=(wide(F32), jax.ShapeDtypeStruct((2, TOK, WP), BF), wide(BF), wide(F32)),
        in_specs=[vm] * 4,
        out_specs=(vm,) * 4,
        scratch_shapes=[pltpu.VMEM((WP, TOK), F32), pltpu.VMEM((W, TOK), F32)],
        compiler_params=pltpu.CompilerParams(vmem_limit_bytes=24 * 2**20),
        cost_estimate=pl.CostEstimate(flops=10**6, bytes_accessed=10**7, transcendentals=0),
    )(state.T, inj.T, cot.T, gain)


PLACE = (0, 2, 6, 4)
ALL = 2 * TOK


def half_of(core):
    return pl.ds(pl.multiple_of(core * HALF, 128), HALF)


def first_kernel(place, acts_ref, peer_ref, *rest):
    pieces = rest[:8]
    s_ref, back_ref, give_ref, w_ref, both_ref, sems = rest[8:]
    px, py, pc = place[0], place[1], place[2]
    copies = []
    for k in range(4):
        for j in range(4):
            sx = jnp.where(pc == 0, px + 4 - j, px + 4 - k) % 4
            sy = jnp.where(pc == 0, py + 4 - k, py + 4 - j) % 4
            row = pl.multiple_of((sy * 4 + sx) * SP, SP)
            src = pieces[PLACE[k] + j // 2].at[j % 2]
            copies.append(pltpu.make_async_copy(src, w_ref.at[pl.ds(row, SP), :], sems.at[len(copies)]))
    for c in copies:
        c.start()
    both_ref[:TOK] = acts_ref[0]
    both_ref[TOK:] = peer_ref[0]
    grads = jnp.concatenate([acts_ref[1, :, half_of(pc)], peer_ref[1, :, half_of(pc)]], axis=0)
    for c in copies:
        c.wait()
    s1 = jnp.dot(both_ref[...], w_ref[...], preferred_element_type=F32)
    s_ref[...] = s1[:TOK]
    give_ref[:, :HALF] = s1[TOK:]
    for t in range(2):
        rows = slice(t * HALF, t * HALF + HALF)
        back = nt(grads, w_ref[rows, :])
        back_ref[:, rows] = back[:TOK]
        give_ref[:, HALF + t * HALF : 2 * HALF + t * HALF] = back[TOK:]


def middle_kernel(place, s_ref, back_ref, got_ref, n0_ref, inj_ref, cot_ref, gain_ref, next_ref, injg_ref, part_ref, s1_ref):
    pc, deep = place[2], place[3] >= 2
    mine, other = half_of(pc), half_of(1 - pc)
    s1_ref[:, mine] = s_ref[...] + inj_ref[:, mine].astype(F32)
    s1_ref[:, other] = got_ref[:, :HALF] + inj_ref[:, other].astype(F32)
    acc = jnp.zeros((TOK, 128), F32)
    for t in range(WP // 128):
        s1 = s1_ref[:, 128 * t : 128 * t + 128]
        acc = acc + s1 * s1
    inv1 = lax.rsqrt(jnp.sum(acc, axis=1, keepdims=True) / W + EPS)

    def second(t, acc):
        cols = pl.ds(pl.multiple_of(t * TILE, TILE), TILE)
        n1 = s1_ref[:, cols] * inv1
        back = back_ref[:, cols] + got_ref[:, pl.ds(pl.multiple_of(HALF + t * TILE, 128), TILE)]
        gain = gain_ref[:, cols]
        next_ref[0, :, cols] = (n1 * gain).astype(BF)
        part_ref[:, cols] = jnp.sum(back * jnp.where(deep, n1, n0_ref[:, cols]), axis=0, keepdims=True)
        return acc + back * gain * n1

    acc = lax.fori_loop(0, WP // TILE, second, jnp.zeros((TOK, TILE), F32))
    mean1 = jnp.sum(acc, axis=1, keepdims=True) / W

    def third(t, carry):
        cols = pl.ds(pl.multiple_of(t * TILE, TILE), TILE)
        n1 = s1_ref[:, cols] * inv1
        back = back_ref[:, cols] + got_ref[:, pl.ds(pl.multiple_of(HALF + t * TILE, 128), TILE)]
        d1 = jnp.where(deep, inv1 * (back * gain_ref[:, cols] - n1 * mean1), 0.0)
        next_ref[1, :, cols] = d1.astype(BF)
        injg_ref[:, cols] = (cot_ref[:, cols] + d1).astype(BF)
        return carry

    lax.fori_loop(0, WP // TILE, third, 0)


def grads_kernel(place, next_ref, peer_ref, n0_ref, n0_peer_ref, part1_ref, w_ref, part_ref):
    pc = place[2]
    grads = jnp.concatenate([next_ref[1, :, half_of(pc)], peer_ref[1, :, half_of(pc)]], axis=0)
    for t in range(2):
        rows = slice(t * HALF, t * HALF + HALF)
        back = nt(grads, w_ref[rows, :])
        sums = jnp.sum(back[:TOK] * n0_ref[:, rows] + back[TOK:] * n0_peer_ref[:, rows], axis=0, keepdims=True)
        part_ref[:, rows] = part1_ref[:, rows] + sums


def state_kernel(next_ref, peer_ref, w_ref, s_ref, give_ref, both_ref):
    both_ref[:TOK] = next_ref[0]
    both_ref[TOK:] = peer_ref[0]
    s2 = jnp.dot(both_ref[...], w_ref[...], preferred_element_type=F32)
    s_ref[...] = s2[:TOK]
    give_ref[...] = s2[TOK:]


VM = pl.BlockSpec(memory_space=pltpu.VMEM)
SM = pl.BlockSpec(memory_space=pltpu.SMEM)
HB = pl.BlockSpec(memory_space=pl.ANY)


def shape(*dims, dtype=F32):
    return jax.ShapeDtypeStruct(dims, dtype)


def first_call(place, acts, peer, pieces):
    return pl.pallas_call(
        first_kernel,
        out_shape=(shape(TOK, HALF), shape(TOK, WP), shape(TOK, HALF + WP), shape(WP, HALF, dtype=BF)),
        in_specs=[SM, VM, VM] + [HB] * 8,
        out_specs=(VM,) * 4,
        scratch_shapes=[pltpu.VMEM((ALL, WP), BF), pltpu.SemaphoreType.DMA((16,))],
        compiler_params=pltpu.CompilerParams(vmem_limit_bytes=24 * 2**20),
        cost_estimate=pl.CostEstimate(flops=8 * TOK * WP * HALF, bytes_accessed=2 * WP * HALF, transcendentals=0),
    )(place, acts, peer, *pieces)


def middle_call(place, s_own, back, got, n0, inj, cot, gain):
    return pl.pallas_call(
        middle_kernel,
        out_shape=(shape(2, TOK, WP, dtype=BF), shape(TOK, WP, dtype=BF), shape(1, WP), shape(TOK, WP)),
        in_specs=[SM] + [VM] * 7,
        out_specs=(VM,) * 4,
        compiler_params=pltpu.CompilerParams(vmem_limit_bytes=20 * 2**20),
        cost_estimate=pl.CostEstimate(flops=20 * TOK * WP, bytes_accessed=10**7, transcendentals=0),
    )(place, s_own, back, got, n0, inj, cot, gain)


def grads_call(place, nexts, peer, n0, n0_peer, part1, w):
    return pl.pallas_call(
        grads_kernel,
        out_shape=shape(1, WP),
        in_specs=[SM] + [VM] * 6,
        out_specs=VM,
        compiler_params=pltpu.CompilerParams(vmem_limit_bytes=24 * 2**20),
        cost_estimate=pl.CostEstimate(flops=4 * TOK * WP * HALF, bytes_accessed=2 * WP * HALF, transcendentals=0),
    )(place, nexts, peer, n0, n0_peer, part1, w)


def state_call(nexts, peer, w):
    return pl.pallas_call(
        state_kernel,
        out_shape=(shape(TOK, HALF), shape(TOK, HALF)),
        in_specs=[VM] * 3,
        out_specs=(VM,) * 2,
        scratch_shapes=[pltpu.VMEM((ALL, WP), BF)],
        compiler_params=pltpu.CompilerParams(vmem_limit_bytes=24 * 2**20),
        cost_estimate=pl.CostEstimate(flops=4 * TOK * WP * HALF, bytes_accessed=2 * WP * HALF, transcendentals=0),
    )(nexts, peer, w)


def tighten(wide_ref, tall_ref, out_ref):
    for s in range(16):
        tall_ref[SH * s : SH * s + SH, :] = wide_ref[SP * s : SP * s + SH, :]
    out_ref[...] = tall_ref[...].astype(BF)


def flip_kernel(rows_ref, out_ref, wide_ref, tall_ref):
    for t in range(WP // 128):
        cols = slice(128 * t, 128 * t + 128)
        wide_ref[cols, :] = rows_ref[:, cols].astype(F32).T
    tighten(wide_ref, tall_ref, out_ref)


def final_kernel(place, s_ref, got_ref, inj_ref, s1_ref, out_ref, s2_ref, wide_ref, tall_ref):
    pc, deep = place[2], place[3] >= 2
    s2_ref[:, half_of(pc)] = s_ref[...]
    s2_ref[:, half_of(1 - pc)] = got_ref[...]
    for t in range(WP // 128):
        cols = slice(128 * t, 128 * t + 128)
        s2 = s2_ref[:, cols] + inj_ref[:, cols].astype(F32)
        wide_ref[cols, :] = jnp.where(deep, s2, s1_ref[:, cols]).T
    tighten(wide_ref, tall_ref, out_ref)


FLIPPED = [pltpu.VMEM((WP, TOK), F32), pltpu.VMEM((W, TOK), F32)]


def flip_call(rows):
    return pl.pallas_call(
        flip_kernel,
        out_shape=shape(W, TOK, dtype=BF),
        in_specs=[VM],
        out_specs=VM,
        scratch_shapes=FLIPPED,
        compiler_params=pltpu.CompilerParams(vmem_limit_bytes=16 * 2**20),
        cost_estimate=pl.CostEstimate(flops=10**6, bytes_accessed=3 * 10**6, transcendentals=0),
    )(rows).T


def final_call(place, s_own, got, inj, s1):
    return pl.pallas_call(
        final_kernel,
        out_shape=shape(W, TOK, dtype=BF),
        in_specs=[SM] + [VM] * 4,
        out_specs=VM,
        scratch_shapes=[pltpu.VMEM((TOK, WP), F32)] + FLIPPED,
        compiler_params=pltpu.CompilerParams(vmem_limit_bytes=16 * 2**20),
        cost_estimate=pl.CostEstimate(flops=10**6, bytes_accessed=5 * 10**6, transcendentals=0),
    )(place, s_own, got, inj, s1).T


def gather(own, acts):
    down = send(own, along(True, -1))
    up = send(own, along(True, 1))
    far = send(own, along(True, 2))
    acts, down, up, far = lax.optimization_barrier((acts, down, up, far))
    low = jnp.stack([own, up])
    high = jnp.stack([far, down])
    low3 = send(low, along(False, -1))
    high1 = send(high, along(False, 1))
    high3 = send(high, along(False, -1))
    low1 = send(low, along(False, 1))
    high2 = send(high3, along(False, -1))
    low2 = send(low1, along(False, 1))
    return acts, (low, high, low1, high1, low3, high3, low2, high2)


def groups(axis):
    found = {}
    for x, y, z, c in chips():
        key = {"z": (x, y, c), "y": (x, z, c), "xc": (y, z)}[axis]
        found.setdefault(key, []).append(line(x, y, z, c))
    return list(found.values())


def spreads(part, axis):
    return lax.all_to_all(jnp.broadcast_to(part, (8, WP)), AXES, 0, 0, axis_index_groups=groups(axis))


def gathered(every):
    return jnp.sum(every.reshape(8, WP), axis=0, keepdims=True)


def shards(state0, injected, core_weight, gain, counts, cotangent):
    dp, fs = lax.axis_index("dp"), lax.axis_index("fsdp")
    pc = dp % 2
    place = jnp.stack([fs % 4, fs // 4, pc, counts[0]]).astype(jnp.int32)
    gain_w = jnp.pad(gain.reshape(16, SH), ((0, 0), (0, SP - SH))).reshape(1, WP)
    acts = prepare(state0, injected, cotangent, gain_w)
    (n0, acts, inj, cot), pieces = gather(spread(place, core_weight), acts)
    peer, n0 = lax.optimization_barrier((send(acts, SWAP), n0))
    peer, n0_peer = lax.optimization_barrier((peer, send(n0, SWAP)))
    s_own, back, give, half = first_call(place, acts, peer, pieces)
    nexts, injg, part1, s1 = middle_call(place, s_own, back, send(give, SWAP), n0, inj, cot, gain_w)
    peer = send(nexts, SWAP)
    part = grads_call(place, nexts, peer, n0, n0_peer, part1, half)
    nexts, peer, part = lax.optimization_barrier((nexts, peer, part))
    every = spreads(part, "z")
    s_own, give = state_call(nexts, peer, half)
    s_own, give, every = lax.optimization_barrier((s_own, give, every))
    got = send(give, SWAP)
    every = spreads(gathered(every), "y")
    got, injg, every = lax.optimization_barrier((got, flip_call(injg), every))
    every = spreads(gathered(every), "xc")
    final = final_call(place, s_own, got, inj, s1)
    return (final, injg, gathered(every).reshape(16, SP)[:, :SH].reshape(W))


def solution(mesh):
    rows = P(AXES, None)
    return jax.shard_map(
        shards,
        mesh=mesh,
        in_specs=(rows, rows, P("fsdp", None), P(), P(AXES), rows),
        out_specs=(rows, rows, P()),
        check_vma=False,
    )
```

```python
import itertools

import jax
import jax.numpy as jnp
from jax import lax
from jax.experimental import pallas as pl
from jax.experimental.pallas import tpu as pltpu
from jax.sharding import PartitionSpec as P

AXES = ("dp", "fsdp")
NX, NY, NZ, NC = 4, 8, 8, 2
YL = 4
W = 2640
SH = 165
SP = 176
WP = 16 * SP
HALF = WP // 2
TOK = 128
TILE = 256
EPS = 1e-06
BF = jnp.bfloat16
F32 = jnp.float32


def line(x, y, z, c):
    x, y, z, c = x % NX, y % NY, z % NZ, c % NC
    return ((y // YL) * NZ * NC + z * NC + c) * 16 + (y % YL) * NX + x


def chips():
    return itertools.product(range(NX), range(NY), range(NZ), range(NC))


def along(first, step):
    pairs = []
    for x, y, z, c in chips():
        in_x = (c == 0) == first
        pairs.append((line(x, y, z, c), line(x + step * in_x, y + step * (not in_x), z, c)))
    return pairs


SWAP = [(line(x, y, z, c), line(x, y, z, 1 - c)) for x, y, z, c in chips()]


def send(array, pairs):
    return lax.ppermute(array, AXES, pairs)


def nt(a, b):
    return lax.dot_general(a, b, (((1,), (1,)), ((), ())), preferred_element_type=F32)


def spread_kernel(place, w_ref, out_ref, wide_ref):
    wide_ref[...] = jnp.zeros_like(wide_ref)
    for t in range(20):
        wide_ref[0:SH, 128 * t : 128 * t + 128] = w_ref[:, 128 * t : 128 * t + 128].astype(F32)
    wide_ref[0:SH, 2560:W] = w_ref[:, 2560:W].astype(F32)
    lane = lax.broadcasted_iota(jnp.int32, (SP, 128), 1)
    for core in range(2):

        @pl.when(place[2] == core)
        def _():
            for t in range(HALF // 128):
                tile = jnp.zeros((SP, 128), F32)
                for j in range(8):
                    low, high = SP * j - 128 * t, SP * j + SH - 128 * t
                    if high <= 0 or low >= 128:
                        continue
                    q = SH * (8 * core + j) - low
                    base = (q // 128) * 128
                    win = wide_ref[:, base : base + 256]
                    moved = pltpu.roll(win, (base - q) % 256, 1)[:, :128]
                    tile = jnp.where((lane >= low) & (lane < high), moved, tile)
                out_ref[:, 128 * t : 128 * t + 128] = tile.astype(BF)

def spread(place, w):
    vm = pl.BlockSpec(memory_space=pltpu.VMEM)
    return pl.pallas_call(
        spread_kernel,
        out_shape=jax.ShapeDtypeStruct((SP, HALF), BF),
        in_specs=[pl.BlockSpec(memory_space=pltpu.SMEM), vm],
        out_specs=vm,
        scratch_shapes=[pltpu.VMEM((SP, 2944), F32)],
        compiler_params=pltpu.CompilerParams(vmem_limit_bytes=16 * 2**20),
    )(place, w)

def prepare_kernel(state_ref, inj_ref, cot_ref, gain_ref, n0_ref, n0b_ref, acts_ref, injw_ref, cotw_ref, wide_ref, tall_ref):
    def regroup(src_ref):
        for s in range(16):
            wide_ref[SP * s : SP * s + SH, :] = src_ref[SH * s : SH * s + SH, :]

    for s in range(16):
        wide_ref[SP * s + SH : SP * s + SP, :] = jnp.zeros((SP - SH, TOK), F32)
    regroup(state_ref)
    acc = jnp.zeros((TOK, 128), F32)
    for t in range(WP // 128):
        cols = slice(128 * t, 128 * t + 128)
        s = wide_ref[cols, :].T
        n0_ref[:, cols] = s
        acc = acc + s * s
    inv = lax.rsqrt(jnp.sum(acc, axis=1, keepdims=True) / W + EPS)
    for t in range(WP // 128):
        cols = slice(128 * t, 128 * t + 128)
        n0 = n0_ref[:, cols] * inv
        n0_ref[:, cols] = n0
        n0b_ref[:, cols] = n0.astype(BF)
        acts_ref[0, :, cols] = (n0 * gain_ref[:, cols]).astype(BF)
    regroup(cot_ref)
    for t in range(WP // 128):
        cols = slice(128 * t, 128 * t + 128)
        c = wide_ref[cols, :].T
        cotw_ref[:, cols] = c
        acts_ref[1, :, cols] = c.astype(BF)
    tall_ref[...] = inj_ref[...].astype(F32)
    regroup(tall_ref)
    for t in range(WP // 128):
        cols = slice(128 * t, 128 * t + 128)
        injw_ref[:, cols] = wide_ref[cols, :].T.astype(BF)

def prepare(state, inj, cot, gain):
    vm = pl.BlockSpec(memory_space=pltpu.VMEM)
    wide = lambda dt: jax.ShapeDtypeStruct((TOK, WP), dt)
    return pl.pallas_call(
        prepare_kernel,
        out_shape=(wide(F32), wide(BF), jax.ShapeDtypeStruct((2, TOK, WP), BF), wide(BF), wide(F32)),
        in_specs=[vm] * 4,
        out_specs=(vm,) * 5,
        scratch_shapes=[pltpu.VMEM((WP, TOK), F32), pltpu.VMEM((W, TOK), F32)],
        compiler_params=pltpu.CompilerParams(vmem_limit_bytes=24 * 2**20),
        cost_estimate=pl.CostEstimate(flops=10**6, bytes_accessed=10**7, transcendentals=0),
    )(state.T, inj.T, cot.T, gain)


PLACE = (0, 2, 6, 4)
ALL = 2 * TOK


def half_of(core):
    return pl.ds(pl.multiple_of(core * HALF, 128), HALF)


def first_kernel(place, acts_ref, peer_ref, *rest):
    pieces = rest[:8]
    s_ref, back_ref, give_ref, w_ref, both_ref, sems = rest[8:]
    px, py, pc = place[0], place[1], place[2]
    copies = []
    for k in range(4):
        for j in range(4):
            sx = jnp.where(pc == 0, px + 4 - j, px + 4 - k) % 4
            sy = jnp.where(pc == 0, py + 4 - k, py + 4 - j) % 4
            row = pl.multiple_of((sy * 4 + sx) * SP, SP)
            src = pieces[PLACE[k] + j // 2].at[j % 2]
            copies.append(pltpu.make_async_copy(src, w_ref.at[pl.ds(row, SP), :], sems.at[len(copies)]))
    for c in copies:
        c.start()
    both_ref[:TOK] = acts_ref[0]
    both_ref[TOK:] = peer_ref[0]
    grads = jnp.concatenate([acts_ref[1, :, half_of(pc)], peer_ref[1, :, half_of(pc)]], axis=0)
    for c in copies:
        c.wait()
    s1 = jnp.dot(both_ref[...], w_ref[...], preferred_element_type=F32)
    s_ref[...] = s1[:TOK]
    give_ref[:, :HALF] = s1[TOK:].astype(BF)
    for t in range(2):
        rows = slice(t * HALF, t * HALF + HALF)
        back = nt(grads, w_ref[rows, :])
        back_ref[:, rows] = back[:TOK]
        give_ref[:, HALF + t * HALF : 2 * HALF + t * HALF] = back[TOK:].astype(BF)


def middle_kernel(place, s_ref, back_ref, got_ref, n0_ref, inj_ref, cot_ref, gain_ref, next_ref, injg_ref, part_ref, s1_out_ref, s1_ref):
    pc, deep = place[2], place[3] >= 2
    mine, other = half_of(pc), half_of(1 - pc)
    s1_ref[:, mine] = s_ref[...] + inj_ref[:, mine].astype(F32)
    s1_ref[:, other] = got_ref[:, :HALF].astype(F32) + inj_ref[:, other].astype(F32)
    acc = jnp.zeros((TOK, 128), F32)
    for t in range(WP // 128):
        s1 = s1_ref[:, 128 * t : 128 * t + 128]
        acc = acc + s1 * s1
    inv1 = lax.rsqrt(jnp.sum(acc, axis=1, keepdims=True) / W + EPS)

    def second(t, acc):
        cols = pl.ds(pl.multiple_of(t * TILE, TILE), TILE)
        n1 = s1_ref[:, cols] * inv1
        back = back_ref[:, cols] + got_ref[:, pl.ds(pl.multiple_of(HALF + t * TILE, 128), TILE)].astype(F32)
        gain = gain_ref[:, cols]
        next_ref[0, :, cols] = (n1 * gain).astype(BF)
        part_ref[:, cols] = jnp.sum(back * jnp.where(deep, n1, n0_ref[:, cols]), axis=0, keepdims=True)
        return acc + back * gain * n1

    acc = lax.fori_loop(0, WP // TILE, second, jnp.zeros((TOK, TILE), F32))
    mean1 = jnp.sum(acc, axis=1, keepdims=True) / W

    def third(t, carry):
        cols = pl.ds(pl.multiple_of(t * TILE, TILE), TILE)
        n1 = s1_ref[:, cols] * inv1
        back = back_ref[:, cols] + got_ref[:, pl.ds(pl.multiple_of(HALF + t * TILE, 128), TILE)].astype(F32)
        d1 = jnp.where(deep, inv1 * (back * gain_ref[:, cols] - n1 * mean1), 0.0)
        next_ref[1, :, cols] = d1.astype(BF)
        injg_ref[:, cols] = (cot_ref[:, cols] + d1).astype(BF)
        s1_out_ref[:, cols] = s1_ref[:, cols].astype(BF)
        return carry

    lax.fori_loop(0, WP // TILE, third, 0)


def grads_kernel(place, next_ref, peer_ref, n0_ref, n0_peer_ref, part1_ref, w_ref, part_ref):
    pc = place[2]
    grads = jnp.concatenate([next_ref[1, :, half_of(pc)], peer_ref[1, :, half_of(pc)]], axis=0)
    for t in range(2):
        rows = slice(t * HALF, t * HALF + HALF)
        back = nt(grads, w_ref[rows, :])
        sums = jnp.sum(back[:TOK] * n0_ref[:, rows] + back[TOK:] * n0_peer_ref[:, rows].astype(F32), axis=0, keepdims=True)
        part_ref[:, rows] = part1_ref[:, rows] + sums


def state_kernel(next_ref, peer_ref, w_ref, s_ref, give_ref, both_ref):
    both_ref[:TOK] = next_ref[0]
    both_ref[TOK:] = peer_ref[0]
    s2 = jnp.dot(both_ref[...], w_ref[...], preferred_element_type=F32)
    s_ref[...] = s2[:TOK]
    give_ref[...] = s2[TOK:]


VM = pl.BlockSpec(memory_space=pltpu.VMEM)
SM = pl.BlockSpec(memory_space=pltpu.SMEM)
HB = pl.BlockSpec(memory_space=pl.ANY)


def shape(*dims, dtype=F32):
    return jax.ShapeDtypeStruct(dims, dtype)


def first_call(place, acts, peer, pieces):
    return pl.pallas_call(
        first_kernel,
        out_shape=(shape(TOK, HALF), shape(TOK, WP), shape(TOK, HALF + WP, dtype=BF), shape(WP, HALF, dtype=BF)),
        in_specs=[SM, VM, VM] + [HB] * 8,
        out_specs=(VM,) * 4,
        scratch_shapes=[pltpu.VMEM((ALL, WP), BF), pltpu.SemaphoreType.DMA((16,))],
        compiler_params=pltpu.CompilerParams(vmem_limit_bytes=24 * 2**20),
        cost_estimate=pl.CostEstimate(flops=8 * TOK * WP * HALF, bytes_accessed=2 * WP * HALF, transcendentals=0),
    )(place, acts, peer, *pieces)


def middle_call(place, s_own, back, got, n0, inj, cot, gain):
    return pl.pallas_call(
        middle_kernel,
        out_shape=(shape(2, TOK, WP, dtype=BF), shape(TOK, WP, dtype=BF), shape(1, WP), shape(TOK, WP, dtype=BF)),
        in_specs=[SM] + [VM] * 7,
        out_specs=(VM,) * 4,
        scratch_shapes=[pltpu.VMEM((TOK, WP), F32)],
        compiler_params=pltpu.CompilerParams(vmem_limit_bytes=20 * 2**20),
        cost_estimate=pl.CostEstimate(flops=20 * TOK * WP, bytes_accessed=10**7, transcendentals=0),
    )(place, s_own, back, got, n0, inj, cot, gain)


def grads_call(place, nexts, peer, n0, n0_peer, part1, w):
    return pl.pallas_call(
        grads_kernel,
        out_shape=shape(1, WP),
        in_specs=[SM] + [VM] * 6,
        out_specs=VM,
        compiler_params=pltpu.CompilerParams(vmem_limit_bytes=24 * 2**20),
        cost_estimate=pl.CostEstimate(flops=4 * TOK * WP * HALF, bytes_accessed=2 * WP * HALF, transcendentals=0),
    )(place, nexts, peer, n0, n0_peer, part1, w)


def state_call(nexts, peer, w):
    return pl.pallas_call(
        state_kernel,
        out_shape=(shape(TOK, HALF), shape(TOK, HALF)),
        in_specs=[VM] * 3,
        out_specs=(VM,) * 2,
        scratch_shapes=[pltpu.VMEM((ALL, WP), BF)],
        compiler_params=pltpu.CompilerParams(vmem_limit_bytes=24 * 2**20),
        cost_estimate=pl.CostEstimate(flops=4 * TOK * WP * HALF, bytes_accessed=2 * WP * HALF, transcendentals=0),
    )(nexts, peer, w)


def tighten(wide_ref, tall_ref, out_ref):
    for s in range(16):
        tall_ref[SH * s : SH * s + SH, :] = wide_ref[SP * s : SP * s + SH, :]
    out_ref[...] = tall_ref[...].astype(BF)


def flip_kernel(rows_ref, out_ref, wide_ref, tall_ref):
    for t in range(WP // 128):
        cols = slice(128 * t, 128 * t + 128)
        wide_ref[cols, :] = rows_ref[:, cols].astype(F32).T
    tighten(wide_ref, tall_ref, out_ref)


def final_kernel(place, s_ref, got_ref, inj_ref, s1_ref, out_ref, s2_ref, wide_ref, tall_ref):
    pc, deep = place[2], place[3] >= 2
    s2_ref[:, half_of(pc)] = s_ref[...]
    s2_ref[:, half_of(1 - pc)] = got_ref[...]
    for t in range(WP // 128):
        cols = slice(128 * t, 128 * t + 128)
        s2 = s2_ref[:, cols] + inj_ref[:, cols].astype(F32)
        wide_ref[cols, :] = jnp.where(deep, s2, s1_ref[:, cols].astype(F32)).T
    tighten(wide_ref, tall_ref, out_ref)


FLIPPED = [pltpu.VMEM((WP, TOK), F32), pltpu.VMEM((W, TOK), F32)]


def flip_call(rows):
    return pl.pallas_call(
        flip_kernel,
        out_shape=shape(W, TOK, dtype=BF),
        in_specs=[VM],
        out_specs=VM,
        scratch_shapes=FLIPPED,
        compiler_params=pltpu.CompilerParams(vmem_limit_bytes=16 * 2**20),
        cost_estimate=pl.CostEstimate(flops=10**6, bytes_accessed=3 * 10**6, transcendentals=0),
    )(rows).T


def final_call(place, s_own, got, inj, s1):
    return pl.pallas_call(
        final_kernel,
        out_shape=shape(W, TOK, dtype=BF),
        in_specs=[SM] + [VM] * 4,
        out_specs=VM,
        scratch_shapes=[pltpu.VMEM((TOK, WP), F32)] + FLIPPED,
        compiler_params=pltpu.CompilerParams(vmem_limit_bytes=16 * 2**20),
        cost_estimate=pl.CostEstimate(flops=10**6, bytes_accessed=5 * 10**6, transcendentals=0),
    )(place, s_own, got, inj, s1).T


def gather(own, acts):
    down = send(own, along(True, -1))
    up = send(own, along(True, 1))
    far = send(own, along(True, 2))
    acts, down, up, far = lax.optimization_barrier((acts, down, up, far))
    low = jnp.stack([own, up])
    high = jnp.stack([far, down])
    low3 = send(low, along(False, -1))
    high1 = send(high, along(False, 1))
    high3 = send(high, along(False, -1))
    low1 = send(low, along(False, 1))
    high2 = send(high3, along(False, -1))
    low2 = send(low1, along(False, 1))
    return acts, (low, high, low1, high1, low3, high3, low2, high2)


def groups(axis):
    found = {}
    for x, y, z, c in chips():
        key = {"z": (x, y, c), "y": (x, z, c), "xc": (y, z)}[axis]
        found.setdefault(key, []).append(line(x, y, z, c))
    return list(found.values())


def spreads(part, axis):
    return lax.all_to_all(jnp.broadcast_to(part, (8, WP)), AXES, 0, 0, axis_index_groups=groups(axis))


def gathered(every):
    return jnp.sum(every.reshape(8, WP), axis=0, keepdims=True)


def shards(state0, injected, core_weight, gain, counts, cotangent):
    dp, fs = lax.axis_index("dp"), lax.axis_index("fsdp")
    pc = dp % 2
    place = jnp.stack([fs % 4, fs // 4, pc, counts[0]]).astype(jnp.int32)
    gain_w = jnp.pad(gain.reshape(16, SH), ((0, 0), (0, SP - SH))).reshape(1, WP)
    acts = prepare(state0, injected, cotangent, gain_w)
    (n0, n0_small, acts, inj, cot), pieces = gather(spread(place, core_weight), acts)
    peer = send(acts, SWAP)
    s_own, back, give, half = first_call(place, acts, peer, pieces)
    n0_small, give = lax.optimization_barrier((n0_small, give))
    n0_peer, got = lax.optimization_barrier((send(n0_small, SWAP), send(give, SWAP)))
    nexts, injg, part1, s1 = middle_call(place, s_own, back, got, n0, inj, cot, gain_w)
    peer = send(nexts, SWAP)
    part = grads_call(place, nexts, peer, n0, n0_peer, part1, half)
    s_own, give = state_call(nexts, peer, half)
    s_own, give, part = lax.optimization_barrier((s_own, give, part))
    part = gathered(spreads(part, "z"))
    give, part = lax.optimization_barrier((give, part))
    got = send(give, SWAP)
    every = spreads(part, "y")
    got, injg, every = lax.optimization_barrier((got, flip_call(injg), every))
    every = spreads(gathered(every), "xc")
    final = final_call(place, s_own, got, inj, s1)
    return (final, injg, gathered(every).reshape(16, SP)[:, :SH].reshape(W))


def solution(mesh):
    rows = P(AXES, None)
    return jax.shard_map(
        shards,
        mesh=mesh,
        in_specs=(rows, rows, P("fsdp", None), P(), P(AXES), rows),
        out_specs=(rows, rows, P()),
        check_vma=False,
    )
```

```python
import itertools

import jax
import jax.numpy as jnp
from jax import lax
from jax.experimental import pallas as pl
from jax.experimental.pallas import tpu as pltpu
from jax.sharding import PartitionSpec as P

AXES = ("dp", "fsdp")
NX, NY, NZ, NC = 4, 8, 8, 2
YL = 4
W = 2640
SH = 165
SP = 176
WP = 16 * SP
HALF = WP // 2
TOK = 128
TILE = 256
EPS = 1e-06
BF = jnp.bfloat16
F32 = jnp.float32


def line(x, y, z, c):
    x, y, z, c = x % NX, y % NY, z % NZ, c % NC
    return ((y // YL) * NZ * NC + z * NC + c) * 16 + (y % YL) * NX + x


def chips():
    return itertools.product(range(NX), range(NY), range(NZ), range(NC))


def along(first, step):
    pairs = []
    for x, y, z, c in chips():
        in_x = (c == 0) == first
        pairs.append((line(x, y, z, c), line(x + step * in_x, y + step * (not in_x), z, c)))
    return pairs


SWAP = [(line(x, y, z, c), line(x, y, z, 1 - c)) for x, y, z, c in chips()]


def send(array, pairs):
    return lax.ppermute(array, AXES, pairs)


def nt(a, b):
    return lax.dot_general(a, b, (((1,), (1,)), ((), ())), preferred_element_type=F32)


def spread_kernel(place, w_ref, out_ref, wide_ref):
    wide_ref[...] = jnp.zeros_like(wide_ref)
    for t in range(20):
        wide_ref[0:SH, 128 * t : 128 * t + 128] = w_ref[:, 128 * t : 128 * t + 128].astype(F32)
    wide_ref[0:SH, 2560:W] = w_ref[:, 2560:W].astype(F32)
    lane = lax.broadcasted_iota(jnp.int32, (SP, 128), 1)
    for core in range(2):

        @pl.when(place[2] == core)
        def _():
            for t in range(HALF // 128):
                tile = jnp.zeros((SP, 128), F32)
                for j in range(8):
                    low, high = SP * j - 128 * t, SP * j + SH - 128 * t
                    if high <= 0 or low >= 128:
                        continue
                    q = SH * (8 * core + j) - low
                    base = (q // 128) * 128
                    win = wide_ref[:, base : base + 256]
                    moved = pltpu.roll(win, (base - q) % 256, 1)[:, :128]
                    tile = jnp.where((lane >= low) & (lane < high), moved, tile)
                out_ref[:, 128 * t : 128 * t + 128] = tile.astype(BF)

def spread(place, w):
    vm = pl.BlockSpec(memory_space=pltpu.VMEM)
    return pl.pallas_call(
        spread_kernel,
        out_shape=jax.ShapeDtypeStruct((SP, HALF), BF),
        in_specs=[pl.BlockSpec(memory_space=pltpu.SMEM), vm],
        out_specs=vm,
        scratch_shapes=[pltpu.VMEM((SP, 2944), F32)],
        compiler_params=pltpu.CompilerParams(vmem_limit_bytes=16 * 2**20),
    )(place, w)

def prepare_kernel(state_ref, inj_ref, cot_ref, gain_ref, n0_ref, n0b_ref, acts_ref, injw_ref, cotw_ref, wide_ref, tall_ref):
    def regroup(src_ref):
        for s in range(16):
            wide_ref[SP * s : SP * s + SH, :] = src_ref[SH * s : SH * s + SH, :]

    for s in range(16):
        wide_ref[SP * s + SH : SP * s + SP, :] = jnp.zeros((SP - SH, TOK), F32)
    regroup(state_ref)
    acc = jnp.zeros((TOK, 128), F32)
    for t in range(WP // 128):
        cols = slice(128 * t, 128 * t + 128)
        s = wide_ref[cols, :].T
        n0_ref[:, cols] = s
        acc = acc + s * s
    inv = lax.rsqrt(jnp.sum(acc, axis=1, keepdims=True) / W + EPS)
    for t in range(WP // 128):
        cols = slice(128 * t, 128 * t + 128)
        n0 = n0_ref[:, cols] * inv
        n0_ref[:, cols] = n0
        n0b_ref[:, cols] = n0.astype(BF)
        acts_ref[0, :, cols] = (n0 * gain_ref[:, cols]).astype(BF)
    regroup(cot_ref)
    for t in range(WP // 128):
        cols = slice(128 * t, 128 * t + 128)
        c = wide_ref[cols, :].T
        cotw_ref[:, cols] = c
        acts_ref[1, :, cols] = c.astype(BF)
    tall_ref[...] = inj_ref[...].astype(F32)
    regroup(tall_ref)
    for t in range(WP // 128):
        cols = slice(128 * t, 128 * t + 128)
        injw_ref[:, cols] = wide_ref[cols, :].T.astype(BF)

def prepare(state, inj, cot, gain):
    vm = pl.BlockSpec(memory_space=pltpu.VMEM)
    wide = lambda dt: jax.ShapeDtypeStruct((TOK, WP), dt)
    return pl.pallas_call(
        prepare_kernel,
        out_shape=(wide(F32), wide(BF), jax.ShapeDtypeStruct((2, TOK, WP), BF), wide(BF), wide(F32)),
        in_specs=[vm] * 4,
        out_specs=(vm,) * 5,
        scratch_shapes=[pltpu.VMEM((WP, TOK), F32), pltpu.VMEM((W, TOK), F32)],
        compiler_params=pltpu.CompilerParams(vmem_limit_bytes=24 * 2**20),
        cost_estimate=pl.CostEstimate(flops=10**6, bytes_accessed=10**7, transcendentals=0),
    )(state.T, inj.T, cot.T, gain)


PLACE = (0, 2, 6, 4)
ALL = 2 * TOK


def half_of(core):
    return pl.ds(pl.multiple_of(core * HALF, 128), HALF)


def first_kernel(place, acts_ref, peer_ref, *rest):
    pieces = rest[:8]
    s_ref, back_ref, give_ref, w_ref, both_ref, sems = rest[8:]
    px, py, pc = place[0], place[1], place[2]
    copies = []
    for k in range(4):
        for j in range(4):
            sx = jnp.where(pc == 0, px + 4 - j, px + 4 - k) % 4
            sy = jnp.where(pc == 0, py + 4 - k, py + 4 - j) % 4
            shard = sy * 4 + sx
            row = pl.multiple_of(shard * SP, SP)
            src = pieces[PLACE[k] + j // 2].at[j % 2]
            copies.append((shard, pltpu.make_async_copy(src, w_ref.at[pl.ds(row, SP), :], sems.at[shard])))
    for late in range(2):
        for shard, copy in copies:
            pl.when(shard // 8 == late)(copy.start)
    both_ref[:TOK] = acts_ref[0]
    both_ref[TOK:] = peer_ref[0]
    grads = jnp.concatenate([acts_ref[1, :, half_of(pc)], peer_ref[1, :, half_of(pc)]], axis=0)
    for t in range(2):
        for shard in range(8 * t, 8 * t + 8):
            pltpu.make_async_copy(pieces[0].at[0], w_ref.at[SP * shard : SP * shard + SP, :], sems.at[shard]).wait()
        rows = slice(t * HALF, t * HALF + HALF)
        back = nt(grads, w_ref[rows, :])
        back_ref[:, rows] = back[:TOK]
        give_ref[:, HALF + t * HALF : 2 * HALF + t * HALF] = back[TOK:].astype(BF)
    s1 = jnp.dot(both_ref[...], w_ref[...], preferred_element_type=F32)
    s_ref[...] = s1[:TOK]
    give_ref[:, :HALF] = s1[TOK:].astype(BF)


def middle_kernel(place, s_ref, back_ref, got_ref, n0_ref, inj_ref, cot_ref, gain_ref, next_ref, injg_ref, part_ref, s1_out_ref, s1_ref):
    pc, deep = place[2], place[3] >= 2
    mine, other = half_of(pc), half_of(1 - pc)
    s1_ref[:, mine] = s_ref[...] + inj_ref[:, mine].astype(F32)
    s1_ref[:, other] = got_ref[:, :HALF].astype(F32) + inj_ref[:, other].astype(F32)
    acc = jnp.zeros((TOK, 128), F32)
    for t in range(WP // 128):
        s1 = s1_ref[:, 128 * t : 128 * t + 128]
        acc = acc + s1 * s1
    inv1 = lax.rsqrt(jnp.sum(acc, axis=1, keepdims=True) / W + EPS)

    def second(t, acc):
        cols = pl.ds(pl.multiple_of(t * TILE, TILE), TILE)
        n1 = s1_ref[:, cols] * inv1
        back = back_ref[:, cols] + got_ref[:, pl.ds(pl.multiple_of(HALF + t * TILE, 128), TILE)].astype(F32)
        gain = gain_ref[:, cols]
        next_ref[0, :, cols] = (n1 * gain).astype(BF)
        part_ref[:, cols] = jnp.sum(back * jnp.where(deep, n1, n0_ref[:, cols]), axis=0, keepdims=True)
        return acc + back * gain * n1

    acc = lax.fori_loop(0, WP // TILE, second, jnp.zeros((TOK, TILE), F32))
    mean1 = jnp.sum(acc, axis=1, keepdims=True) / W

    def third(t, carry):
        cols = pl.ds(pl.multiple_of(t * TILE, TILE), TILE)
        n1 = s1_ref[:, cols] * inv1
        back = back_ref[:, cols] + got_ref[:, pl.ds(pl.multiple_of(HALF + t * TILE, 128), TILE)].astype(F32)
        d1 = jnp.where(deep, inv1 * (back * gain_ref[:, cols] - n1 * mean1), 0.0)
        next_ref[1, :, cols] = d1.astype(BF)
        injg_ref[:, cols] = (cot_ref[:, cols] + d1).astype(BF)
        s1_out_ref[:, cols] = s1_ref[:, cols].astype(BF)
        return carry

    lax.fori_loop(0, WP // TILE, third, 0)


def grads_kernel(place, next_ref, peer_ref, n0_ref, n0_peer_ref, part1_ref, w_ref, part_ref):
    pc = place[2]
    grads = jnp.concatenate([next_ref[1, :, half_of(pc)], peer_ref[1, :, half_of(pc)]], axis=0)
    for t in range(2):
        rows = slice(t * HALF, t * HALF + HALF)
        back = nt(grads, w_ref[rows, :])
        sums = jnp.sum(back[:TOK] * n0_ref[:, rows] + back[TOK:] * n0_peer_ref[:, rows].astype(F32), axis=0, keepdims=True)
        part_ref[:, rows] = part1_ref[:, rows] + sums


def state_kernel(next_ref, peer_ref, w_ref, s_ref, give_ref, both_ref):
    both_ref[:TOK] = next_ref[0]
    both_ref[TOK:] = peer_ref[0]
    s2 = jnp.dot(both_ref[...], w_ref[...], preferred_element_type=F32)
    s_ref[...] = s2[:TOK]
    give_ref[...] = s2[TOK:]


VM = pl.BlockSpec(memory_space=pltpu.VMEM)
SM = pl.BlockSpec(memory_space=pltpu.SMEM)
HB = pl.BlockSpec(memory_space=pl.ANY)


def shape(*dims, dtype=F32):
    return jax.ShapeDtypeStruct(dims, dtype)


def first_call(place, acts, peer, pieces):
    return pl.pallas_call(
        first_kernel,
        out_shape=(shape(TOK, HALF), shape(TOK, WP), shape(TOK, HALF + WP, dtype=BF), shape(WP, HALF, dtype=BF)),
        in_specs=[SM, VM, VM] + [HB] * 8,
        out_specs=(VM,) * 4,
        scratch_shapes=[pltpu.VMEM((ALL, WP), BF), pltpu.SemaphoreType.DMA((16,))],
        compiler_params=pltpu.CompilerParams(vmem_limit_bytes=24 * 2**20),
        cost_estimate=pl.CostEstimate(flops=8 * TOK * WP * HALF, bytes_accessed=2 * WP * HALF, transcendentals=0),
    )(place, acts, peer, *pieces)


def middle_call(place, s_own, back, got, n0, inj, cot, gain):
    return pl.pallas_call(
        middle_kernel,
        out_shape=(shape(2, TOK, WP, dtype=BF), shape(TOK, WP, dtype=BF), shape(1, WP), shape(TOK, WP, dtype=BF)),
        in_specs=[SM] + [VM] * 7,
        out_specs=(VM,) * 4,
        scratch_shapes=[pltpu.VMEM((TOK, WP), F32)],
        compiler_params=pltpu.CompilerParams(vmem_limit_bytes=20 * 2**20),
        cost_estimate=pl.CostEstimate(flops=20 * TOK * WP, bytes_accessed=10**7, transcendentals=0),
    )(place, s_own, back, got, n0, inj, cot, gain)


def grads_call(place, nexts, peer, n0, n0_peer, part1, w):
    return pl.pallas_call(
        grads_kernel,
        out_shape=shape(1, WP),
        in_specs=[SM] + [VM] * 6,
        out_specs=VM,
        compiler_params=pltpu.CompilerParams(vmem_limit_bytes=24 * 2**20),
        cost_estimate=pl.CostEstimate(flops=4 * TOK * WP * HALF, bytes_accessed=2 * WP * HALF, transcendentals=0),
    )(place, nexts, peer, n0, n0_peer, part1, w)


def state_call(nexts, peer, w):
    return pl.pallas_call(
        state_kernel,
        out_shape=(shape(TOK, HALF), shape(TOK, HALF)),
        in_specs=[VM] * 3,
        out_specs=(VM,) * 2,
        scratch_shapes=[pltpu.VMEM((ALL, WP), BF)],
        compiler_params=pltpu.CompilerParams(vmem_limit_bytes=24 * 2**20),
        cost_estimate=pl.CostEstimate(flops=4 * TOK * WP * HALF, bytes_accessed=2 * WP * HALF, transcendentals=0),
    )(nexts, peer, w)


def tighten(wide_ref, tall_ref, out_ref):
    for s in range(16):
        tall_ref[SH * s : SH * s + SH, :] = wide_ref[SP * s : SP * s + SH, :]
    out_ref[...] = tall_ref[...].astype(BF)


def flip_kernel(rows_ref, out_ref, wide_ref, tall_ref):
    for t in range(WP // 128):
        cols = slice(128 * t, 128 * t + 128)
        wide_ref[cols, :] = rows_ref[:, cols].astype(F32).T
    tighten(wide_ref, tall_ref, out_ref)


def final_kernel(place, s_ref, got_ref, inj_ref, s1_ref, out_ref, s2_ref, wide_ref, tall_ref):
    pc, deep = place[2], place[3] >= 2
    s2_ref[:, half_of(pc)] = s_ref[...]
    s2_ref[:, half_of(1 - pc)] = got_ref[...]
    for t in range(WP // 128):
        cols = slice(128 * t, 128 * t + 128)
        s2 = s2_ref[:, cols] + inj_ref[:, cols].astype(F32)
        wide_ref[cols, :] = jnp.where(deep, s2, s1_ref[:, cols].astype(F32)).T
    tighten(wide_ref, tall_ref, out_ref)


FLIPPED = [pltpu.VMEM((WP, TOK), F32), pltpu.VMEM((W, TOK), F32)]


def flip_call(rows):
    return pl.pallas_call(
        flip_kernel,
        out_shape=shape(W, TOK, dtype=BF),
        in_specs=[VM],
        out_specs=VM,
        scratch_shapes=FLIPPED,
        compiler_params=pltpu.CompilerParams(vmem_limit_bytes=16 * 2**20),
        cost_estimate=pl.CostEstimate(flops=10**6, bytes_accessed=3 * 10**6, transcendentals=0),
    )(rows).T


def final_call(place, s_own, got, inj, s1):
    return pl.pallas_call(
        final_kernel,
        out_shape=shape(W, TOK, dtype=BF),
        in_specs=[SM] + [VM] * 4,
        out_specs=VM,
        scratch_shapes=[pltpu.VMEM((TOK, WP), F32)] + FLIPPED,
        compiler_params=pltpu.CompilerParams(vmem_limit_bytes=16 * 2**20),
        cost_estimate=pl.CostEstimate(flops=10**6, bytes_accessed=5 * 10**6, transcendentals=0),
    )(place, s_own, got, inj, s1).T


def gather(own, acts):
    down = send(own, along(True, -1))
    up = send(own, along(True, 1))
    far = send(own, along(True, 2))
    acts, down, up, far = lax.optimization_barrier((acts, down, up, far))
    low = jnp.stack([own, up])
    high = jnp.stack([far, down])
    low3 = send(low, along(False, -1))
    high1 = send(high, along(False, 1))
    high3 = send(high, along(False, -1))
    low1 = send(low, along(False, 1))
    high2 = send(high3, along(False, -1))
    low2 = send(low1, along(False, 1))
    return acts, (low, high, low1, high1, low3, high3, low2, high2)


def groups(axis):
    found = {}
    for x, y, z, c in chips():
        key = {"z": (x, y, c), "y": (x, z, c), "xc": (y, z)}[axis]
        found.setdefault(key, []).append(line(x, y, z, c))
    return list(found.values())


def spreads(part, axis):
    return lax.all_to_all(jnp.broadcast_to(part, (8, WP)), AXES, 0, 0, axis_index_groups=groups(axis))


def gathered(every):
    return jnp.sum(every.reshape(8, WP), axis=0, keepdims=True)


def shards(state0, injected, core_weight, gain, counts, cotangent):
    dp, fs = lax.axis_index("dp"), lax.axis_index("fsdp")
    pc = dp % 2
    place = jnp.stack([fs % 4, fs // 4, pc, counts[0]]).astype(jnp.int32)
    gain_w = jnp.pad(gain.reshape(16, SH), ((0, 0), (0, SP - SH))).reshape(1, WP)
    acts = prepare(state0, injected, cotangent, gain_w)
    (n0, n0_small, acts, inj, cot), pieces = gather(spread(place, core_weight), acts)
    peer = send(acts, SWAP)
    s_own, back, give, half = first_call(place, acts, peer, pieces)
    n0_small, give = lax.optimization_barrier((n0_small, give))
    n0_peer, got = lax.optimization_barrier((send(n0_small, SWAP), send(give, SWAP)))
    nexts, injg, part1, s1 = middle_call(place, s_own, back, got, n0, inj, cot, gain_w)
    peer = send(nexts, SWAP)
    part = grads_call(place, nexts, peer, n0, n0_peer, part1, half)
    s_own, give = state_call(nexts, peer, half)
    s_own, give, part = lax.optimization_barrier((s_own, give, part))
    part = gathered(spreads(part, "z"))
    give, part = lax.optimization_barrier((give, part))
    got = send(give, SWAP)
    every = spreads(part, "y")
    got, injg, every = lax.optimization_barrier((got, flip_call(injg), every))
    every = spreads(gathered(every), "xc")
    final = final_call(place, s_own, got, inj, s1)
    return (final, injg, gathered(every).reshape(16, SP)[:, :SH].reshape(W))


def solution(mesh):
    rows = P(AXES, None)
    return jax.shard_map(
        shards,
        mesh=mesh,
        in_specs=(rows, rows, P("fsdp", None), P(), P(AXES), rows),
        out_specs=(rows, rows, P()),
        check_vma=False,
    )
```
